32 devices in a mesh: dp: 2 (over core), expert: 4 (over y, x), blk: 4 (over z).
Axes of the slice: x: 2, y: 2, z: 4, core: 2. Of those that a mesh axis runs over, the one named last changes fastest.
Arguments:
- tokens: bfloat16 [256, 6144], P('dp', 'blk'), may hold values from -6 to 6
- expert_ids: int32 [256, 2], P('dp'), may hold values from 0 to 7, all different within a row; in each aligned block of 128 rows (0 to 127, 128 to 255, ...) at most 48 rows name the same one
- route_weights: float32 [256, 2], P('dp'), may hold values from 0.1 to 1
- gate_weight: bfloat16 [8, 6144, 8192], P('expert', 'blk', 'dp'), may hold values from -0.078125 to 0.078125
- up_weight: bfloat16 [8, 6144, 8192], P('expert', 'blk', 'dp'), may hold values from -0.078125 to 0.078125
- down_weight: bfloat16 [8, 8192, 6144], P('expert', 'dp', 'blk'), may hold values from -0.0625 to 0.0625
Outputs:
- mixed: bfloat16 [256, 6144], P('dp', 'blk')
The draws below stay inside these ranges and needn't reach their ends.
Inputs may be any that keep to these rules, and one draw needn't show every extreme that they name: `expert_ids`: each row names 2 different experts. Among the 128 rows of one data shard no expert is named more than 48 times, and in every draw some expert is named exactly 48 times in some shard.
All inputs are finite; a program needn't handle non-finite values.
Results may differ from the reference program's by a relative error of at most 0.0051.
Values may be sent and summed in bfloat16 or wider, within the bound.
No kernel may reach another device: no remote copies, remote signals or barrier semaphores. Data moves between devices by JAX's collectives and lax.ppermute only.
A program may use at most 128 MiB of HBM per device.

```python
import math
import jax
import jax.numpy as jnp
import numpy as np
from jax import lax

D = 6144
EXPERTS = 8
FFW = 8192
TOP = 2
TOK_DEV = 128
CAP = 48
TOKENS = 256
N_DP = 2


def block_levels(key, dims, split, low, top_value):
    level, own = 1.0, jax.random.fold_in(key, 6)
    for axis_at, blocks in split:
        steps = jnp.exp(jax.random.uniform(jax.random.fold_in(own, axis_at), (blocks,), jnp.float32, low / len(split), top_value / len(split)))
        level = level * jnp.repeat(steps, dims[axis_at] // blocks).reshape([-1 if axis == axis_at else 1 for axis in range(len(dims))])
    return level


def routed_block(rng, own, number, rows, amount, top, limit, skew):
    order = jax.random.permutation(rng, amount)
    heavy_load, ordinary = load_shares(amount, rows * top, limit, skew, True), load_shares(amount, rows * top, limit, skew, False)
    places = jnp.arange(amount)

    def named(tallies, turn):
        used = int((tallies > 0).sum())
        fixed = max(1, used // 4)
        passed = fixed + (places - fixed + turn * (used - fixed)) % max(1, amount - fixed)
        return jnp.zeros((amount,), jnp.int32).at[order[jnp.where(places < fixed, places, passed)]].set(jnp.asarray(tallies, jnp.int32))

    tallies = jnp.where(number % 4 == 0, named(heavy_load, number // 4), named(ordinary, number - number // 4 - 1))
    mixed = jax.random.permutation(jax.random.fold_in(own, 3), amount)
    source_of, sink = mixed[0:amount // 2 * 2:2], mixed[1:amount // 2 * 2:2]
    room = jnp.minimum(tallies[source_of] - 1, limit - tallies[sink]) // 2
    room = jnp.where((source_of == order[0]) | (sink == order[0]) | (tallies[sink] == 0), 0, jnp.maximum(room, 0))
    passed = jax.random.randint(jax.random.fold_in(own, 4), (amount // 2,), 0, 1 << 20) % (room + 1)
    tallies = tallies.at[source_of].add(-passed).at[sink].add(passed)
    labels = jnp.searchsorted(jnp.cumsum(tallies), jnp.arange(rows * top), side="right").astype(jnp.int32)
    grid = labels.reshape(top, rows).T
    grid = grid[jax.random.permutation(jax.random.fold_in(own, 1), rows)]
    turn = jax.random.randint(jax.random.fold_in(own, 2), (rows, 1), 0, top)
    return jnp.take_along_axis(grid, (jnp.arange(top)[None, :] + turn) % top, axis=1)


def load_shares(amount, total, bound, lean, full):
    loads = [(1 << 20) // math.isqrt(standing ** lean) + 1 for standing in range(1, amount + 1)]
    largest = bound if full else min(bound, max(-(-total // amount), total * loads[0] // sum(loads)))
    least = 1 if total - largest >= amount - 1 else 0
    holding, rest = [largest] + [least] * (amount - 1), total - largest - least * (amount - 1)
    while rest > 0:
        free = [i for i in range(1, amount) if holding[i] < largest] or [i for i in range(1, amount) if holding[i] < bound]
        whole, left = sum([loads[i] for i in free]), rest
        for i in free:
            extra = min(bound - holding[i], max(1, left * loads[i] // whole), rest)
            holding[i] = holding[i] + extra
            rest = rest - extra
    return np.array(holding)


def normal_values(stream_key, extent, spread, most, cuts=(), held_as=jnp.bfloat16):
    result = jax.random.normal(stream_key, extent, jnp.float32) * spread
    if len(cuts) > 0:
        result = block_levels(stream_key, extent, cuts, -0.22, 0.18) * result
    return jnp.clip(result, min=-most, max=most).astype(held_as)


def setup_inputs(seed: int = 0) -> dict:
    key_of = jax.random.split(jax.random.key(seed), 7)
    tokens = normal_values(key_of[0], (TOKENS, D), 1.0, 6.0, ((0, 2), (1, 4)))
    expert_ids_keys = jax.random.split(jax.random.fold_in(key_of[1], 1), TOKENS // TOK_DEV)
    expert_ids_turns = jax.random.permutation(jax.random.fold_in(key_of[1], 3), TOKENS // TOK_DEV)
    expert_ids = jax.vmap(lambda own, number: routed_block(jax.random.fold_in(key_of[1], 2), own, number, TOK_DEV, EXPERTS, TOP, CAP, 2))(expert_ids_keys, expert_ids_turns).reshape((TOKENS, TOP))
    route_weights = jnp.clip(0.1 + 0.9 * jax.random.uniform(key_of[2], (TOKENS, TOP), jnp.float32) ** block_levels(key_of[2], (TOKENS, TOP), ((0, 2),), -0.2, 0.2), 0.1, 1.0)
    gate_weight = normal_values(key_of[3], (EXPERTS, D, FFW), D ** -0.5, 0.078125, ((0, 4), (1, 4), (2, 2)))
    up_weight = normal_values(key_of[4], (EXPERTS, D, FFW), D ** -0.5, 0.078125, ((0, 4), (1, 4), (2, 2)))
    down_weight = normal_values(key_of[5], (EXPERTS, FFW, D), FFW ** -0.5, 0.0625, ((0, 4), (1, 2), (2, 4)))
    return {"tokens": tokens, "expert_ids": expert_ids, "route_weights": route_weights, "gate_weight": gate_weight, "up_weight": up_weight, "down_weight": down_weight}


def reference(tokens, expert_ids, route_weights, gate_weight, up_weight, down_weight):
    shards = N_DP
    flat_ids = expert_ids.reshape(shards, TOK_DEV * TOP)
    one_hot = (flat_ids[:, :, None] == jnp.arange(EXPERTS, dtype=jnp.int32)[None, None, :]).astype(jnp.int32)
    before = jnp.cumsum(one_hot, axis=1) - one_hot
    position = jnp.sum(before * one_hot, axis=2)
    weights = route_weights.reshape(shards, TOK_DEV, TOP)
    token_blocks = tokens.reshape(shards, TOK_DEV, D).astype(jnp.float32)
    slot_ids = jnp.arange(CAP, dtype=jnp.int32)

    def one_expert(accumulated, expert):
        slot_hit = (flat_ids == expert)[:, :, None] & (position[:, :, None] == slot_ids[None, None, :])
        slot_hit = slot_hit.reshape(shards, TOK_DEV, TOP, CAP)
        dispatch = jnp.any(slot_hit, axis=2).astype(jnp.float32)
        combine = jnp.sum(slot_hit.astype(jnp.float32) * weights[:, :, :, None], axis=2)
        picked = jnp.einsum("stc,std->scd", dispatch, token_blocks, precision=lax.Precision.HIGHEST).astype(jnp.bfloat16)
        picked = picked.reshape(shards * CAP, D)
        gate = jnp.dot(picked, lax.dynamic_index_in_dim(gate_weight, expert, 0, keepdims=False), preferred_element_type=jnp.float32)
        up = jnp.dot(picked, lax.dynamic_index_in_dim(up_weight, expert, 0, keepdims=False), preferred_element_type=jnp.float32)
        hidden = (jax.nn.silu(gate) * up).astype(jnp.bfloat16)
        expert_out = jnp.dot(hidden, lax.dynamic_index_in_dim(down_weight, expert, 0, keepdims=False), preferred_element_type=jnp.float32)
        expert_out = expert_out.reshape(shards, CAP, D)
        accumulated = accumulated + jnp.einsum("stc,scd->std", combine, expert_out, precision=lax.Precision.HIGHEST)
        return accumulated, None

    start_sum = jnp.zeros((shards, TOK_DEV, D), jnp.float32)
    summed, unused = lax.scan(one_expert, start_sum, jnp.arange(EXPERTS, dtype=jnp.int32))
    return summed.reshape(TOKENS, D).astype(jnp.bfloat16)
```

```python
import functools

import jax
import jax.numpy as jnp
from jax import lax
from jax.experimental import pallas as pl
from jax.experimental.pallas import tpu as pltpu
from jax.sharding import PartitionSpec as P

CAP = 48
CHUNKS = 4
VMEM_LIMIT = 40 * 1024 * 1024
F32, BF16 = jnp.float32, jnp.bfloat16


def params(steps):
    return pltpu.CompilerParams(
        dimension_semantics=("arbitrary",) * steps, vmem_limit_bytes=VMEM_LIMIT
    )


def slot_hits(ids, group, local_count):
    rows, lanes = ids.shape[0], local_count * CAP
    lane = lax.broadcasted_iota(jnp.int32, (rows, lanes), 1)
    expert = jnp.full((rows, lanes), group * local_count, jnp.int32)
    slot = lane
    for step in range(1, local_count):
        expert = expert + (lane >= step * CAP).astype(jnp.int32)
        slot = slot - CAP * (lane >= step * CAP).astype(jnp.int32)
    named = [ids[:, k : k + 1] == expert for k in range(ids.shape[1])]
    member = functools.reduce(jnp.logical_or, named)
    earlier = lax.broadcasted_iota(jnp.int32, (rows, rows), 1) < lax.broadcasted_iota(
        jnp.int32, (rows, rows), 0
    )
    position = jnp.dot(
        earlier.astype(F32).astype(BF16),
        member.astype(F32).astype(BF16),
        preferred_element_type=F32,
    )
    hit = member & (position.astype(jnp.int32) == slot)
    return hit, named


def pick_kernel(local_count, group_ref, *refs):
    pairs, out_ref = refs[:-1], refs[-1]
    for s in range(len(pairs) // 2):
        ids_ref, tokens_ref = pairs[2 * s], pairs[2 * s + 1]
        hit, _ = slot_hits(ids_ref[...], group_ref[0], local_count)
        rows = lax.dot_general(
            hit.astype(F32).astype(BF16),
            tokens_ref[...],
            (((0,), (0,)), ((), ())),
            preferred_element_type=F32,
        ).astype(BF16)
        for e in range(local_count):
            out_ref[e, s * CAP : (s + 1) * CAP, :] = rows[e * CAP : (e + 1) * CAP, :]


def pick(group, pairs, local_count):
    shards, width = len(pairs) // 2, pairs[1].shape[1]
    return pl.pallas_call(
        functools.partial(pick_kernel, local_count),
        out_shape=jax.ShapeDtypeStruct((local_count, shards * CAP, width), BF16),
        in_specs=[pl.BlockSpec(memory_space=pltpu.SMEM)]
        + [pl.BlockSpec(memory_space=pltpu.VMEM)] * len(pairs),
        out_specs=pl.BlockSpec(memory_space=pltpu.VMEM),
        compiler_params=params(0),
        name="pick",
    )(group, *pairs)


def gate_up_kernel(steps, where_ref, x_ref, gate_ref, up_ref, full_ref, *short_ref):
    step = pl.program_id(1)
    parts = [
        jnp.dot(x_ref[0], w_ref[0], preferred_element_type=F32) for w_ref in (gate_ref, up_ref)
    ]

    @pl.when(step == 0)
    def _():
        for i in range(2):
            full_ref[i, 0] = parts[i]

    @pl.when(step > 0)
    def _():
        for i in range(2):
            full_ref[i, 0] += parts[i]

    if short_ref:

        @pl.when(step == steps - 1)
        def _():
            short_ref[0][...] = full_ref[...].astype(BF16)


def gate_up(where, rows, gate_weight, up_weight, chunk, width, short):
    local_count, count, depth = rows.shape
    chunks = gate_weight.shape[2] // 2 // width
    steps = 2
    weight = pl.BlockSpec(
        (1, depth // steps, width), lambda e, k, where: (e, k, where[0] * chunks + chunk)
    )
    out = pl.BlockSpec((2, 1, count, width), lambda e, k, where: (0, e, 0, 0))
    shape = (2, local_count, count, width)
    return pl.pallas_call(
        functools.partial(gate_up_kernel, steps),
        grid_spec=pltpu.PrefetchScalarGridSpec(
            num_scalar_prefetch=1,
            grid=(local_count, steps),
            in_specs=[
                pl.BlockSpec((1, count, depth // steps), lambda e, k, where: (e, 0, k)),
                weight,
                weight,
            ],
            out_specs=[out] * (1 + short),
        ),
        out_shape=[jax.ShapeDtypeStruct(shape, F32), jax.ShapeDtypeStruct(shape, BF16)][: 1 + short],
        cost_estimate=pl.CostEstimate(
            flops=4 * local_count * count * depth * width,
            bytes_accessed=4 * local_count * depth * width,
            transcendentals=0,
        ),
        compiler_params=params(2),
        name="gate_up",
    )(where, rows, gate_weight, up_weight)


def down_kernel(parts, first, where_ref, *refs):
    refs = list(refs)
    out_ref = refs.pop()
    step = pl.program_id(1)
    total = None
    for i in range(parts):
        at_end, inside, weight = refs[3 * i : 3 * i + 3]
        hidden = jnp.where(where_ref[0] == 1, at_end[0], inside[0])
        product = jnp.dot(hidden, weight[0], preferred_element_type=F32)
        total = product if total is None else total + product

    @pl.when(step == 0)
    def _():
        out_ref[0] = total if first else refs[-1][0] + total

    @pl.when(step > 0)
    def _():
        out_ref[0] += total


def down(where, parts, down_weight, total):
    local_count, count, width = parts[0][0].shape
    features = down_weight.shape[2]
    chunks = down_weight.shape[1] // 2 // width
    steps = 2 if width % 256 == 0 else 1
    operands, specs = [], []
    for at_end, inside, half_at, chunk in parts:
        hidden = pl.BlockSpec((1, count, width // steps), lambda e, k, where: (e, 0, k))
        operands += [at_end, inside, down_weight]
        specs += [
            hidden,
            hidden,
            pl.BlockSpec(
                (1, width // steps, features),
                lambda e, k, where, half_at=half_at, chunk=chunk: (
                    e,
                    (where[half_at] * chunks + chunk) * steps + k,
                    0,
                ),
            ),
        ]
    out = pl.BlockSpec((1, count, features), lambda e, k, where: (e, 0, 0))
    first = total is None
    if not first:
        operands.append(total)
        specs.append(out)
    return pl.pallas_call(
        functools.partial(down_kernel, len(parts), first),
        grid_spec=pltpu.PrefetchScalarGridSpec(
            num_scalar_prefetch=1, grid=(local_count, steps), in_specs=specs, out_specs=out
        ),
        out_shape=jax.ShapeDtypeStruct((local_count, count, features), F32),
        input_output_aliases={} if first else {len(operands): 0},
        cost_estimate=pl.CostEstimate(
            flops=2 * len(parts) * local_count * count * features * width,
            bytes_accessed=2 * len(parts) * local_count * features * width,
            transcendentals=0,
        ),
        compiler_params=params(2),
        name="down",
    )(where, *operands)


def combine_kernel(local_count, groups, group_ref, ids_ref, weights_ref, *refs):
    sums, own_ref, sent = refs[: -groups], refs[-groups], refs[1 - groups :]
    hit, named = slot_hits(ids_ref[...], group_ref[0], local_count)
    scale = sum(
        jnp.where(named[k], weights_ref[:, k : k + 1], 0.0) for k in range(len(named))
    )
    scale = jnp.where(hit, scale, 0.0)
    scale_high = scale.astype(BF16)
    scale_low = (scale - scale_high.astype(F32)).astype(BF16)
    rows = jnp.concatenate(
        [functools.reduce(jnp.add, [ref[e] for ref in sums]) for e in range(local_count)], axis=0
    )
    rows_high = rows.astype(BF16)
    rows_low = (rows - rows_high.astype(F32)).astype(BF16)
    mixed = (
        jnp.dot(scale_high, rows_high, preferred_element_type=F32)
        + jnp.dot(scale_high, rows_low, preferred_element_type=F32)
        + jnp.dot(scale_low, rows_high, preferred_element_type=F32)
    )
    block = own_ref.shape[0]
    for place in range(groups):
        piece = mixed[place * block : (place + 1) * block]
        step = group_ref[0] ^ place

        @pl.when(step == 0)
        def _():
            own_ref[...] = piece

        for other in range(1, groups):

            @pl.when(step == other)
            def _():
                sent[other - 1][...] = piece.astype(BF16)


def combine(group, ids, weights, sums, groups):
    local_count, _, features = sums[0].shape
    block = ids.shape[0] // groups
    return pl.pallas_call(
        functools.partial(combine_kernel, local_count, groups),
        out_shape=[jax.ShapeDtypeStruct((block, features), F32)]
        + [jax.ShapeDtypeStruct((block, features), BF16)] * (groups - 1),
        in_specs=[pl.BlockSpec(memory_space=pltpu.SMEM)]
        + [pl.BlockSpec(memory_space=pltpu.VMEM)] * (2 + len(sums)),
        out_specs=[pl.BlockSpec(memory_space=pltpu.VMEM)] * groups,
        compiler_params=params(0),
        name="combine",
    )(group, ids, weights, *sums)


def gather_kernel(group_ref, *refs):
    out_ref = refs[-1]
    block = refs[0].shape[0]
    for step, piece_ref in enumerate(refs[:-1]):
        start = pl.multiple_of((group_ref[0] ^ step) * block, block)
        out_ref[pl.ds(start, block), :] = piece_ref[...]


def place_blocks(group, pieces):
    block, features = pieces[0].shape
    return pl.pallas_call(
        gather_kernel,
        out_shape=jax.ShapeDtypeStruct((block * len(pieces), features), BF16),
        in_specs=[pl.BlockSpec(memory_space=pltpu.SMEM)]
        + [pl.BlockSpec(memory_space=pltpu.VMEM)] * len(pieces),
        out_specs=pl.BlockSpec(memory_space=pltpu.VMEM),
        compiler_params=params(0),
        name="place_blocks",
    )(group, *pieces)


def local(mesh_shape, tokens, expert_ids, route_weights, gate_weight, up_weight, down_weight):
    shards, groups, line = mesh_shape["dp"], mesh_shape["expert"], mesh_shape["blk"]
    local_count, _, hidden_count = gate_weight.shape
    group = lax.axis_index("expert").astype(jnp.int32).reshape(1)
    place = lax.axis_index("blk")
    at_end = (place == 0) | (place == line - 1)
    far = (place < line // 2).astype(jnp.int32)
    near = 1 - far
    where_far, where_near = far.reshape(1), near.reshape(1)
    where = jnp.stack([at_end.astype(jnp.int32), near, far])

    if shards == 2:
        swap = [(0, 1), (1, 0)]
        other_ids = lax.ppermute(expert_ids, "dp", swap)
        other_tokens = lax.ppermute(tokens, "dp", swap)
        rows = pick(group, [expert_ids, tokens, other_ids, other_tokens], local_count)
    else:
        rows = lax.all_gather(
            pick(group, [expert_ids, tokens], local_count), "dp", axis=1, tiled=True
        )

    hop_pairs = [[(0, 1), (3, 2)], [(1, 2), (2, 1)], [(2, 3), (1, 0)]]
    hop = [functools.partial(lax.ppermute, axis_name="blk", perm=pairs) for pairs in hop_pairs]
    width = max(128, hidden_count // 2 // CHUNKS)
    chunks = hidden_count // 2 // width
    total, before = None, None
    for c in range(chunks):
        far_full, far_short = gate_up(where_far, rows, gate_weight, up_weight, c, width, True)
        (near_full,) = gate_up(where_near, rows, gate_weight, up_weight, c, width, False)
        got = hop[0](far_short)
        got = hop[1]((far_full + got.astype(F32)).astype(BF16))
        got = hop[2]((near_full + got.astype(F32)).astype(BF16))
        summed = near_full + got.astype(F32)
        hidden = (jax.nn.silu(summed[0]) * summed[1]).astype(BF16)
        first = hop[0](hidden)
        second = hop[1](first)
        third = hop[2](second)
        parts = [(hidden, first, 1, c)] + ([before] if before else [])
        total = down(where, parts, down_weight, total)
        before = (third, second, 2, c)
    total = down(where, [before], down_weight, total)

    if shards == 2:
        sums = [total[:, :CAP], lax.ppermute(total[:, CAP:], "dp", swap)]
    else:
        sums = [lax.psum_scatter(total, "dp", scatter_dimension=1, tiled=True)]
    own, *sent = combine(group, expert_ids, route_weights, sums, groups)
    for step in range(1, groups):
        exchange = [(i, i ^ step) for i in range(groups)]
        own = own + lax.ppermute(sent[step - 1], "expert", exchange).astype(F32)
    block = own.astype(BF16)
    pieces = [block]
    for step in range(1, groups):
        pieces.append(lax.ppermute(block, "expert", [(i, i ^ step) for i in range(groups)]))
    return place_blocks(group, pieces)


def solution(mesh):
    placed = (
        P("dp", "blk"),
        P("dp", None),
        P("dp", None),
        P("expert", "blk", "dp"),
        P("expert", "blk", "dp"),
        P("expert", "dp", "blk"),
    )
    return jax.shard_map(
        functools.partial(local, dict(mesh.shape)),
        mesh=mesh,
        in_specs=placed,
        out_specs=P("dp", "blk"),
        check_vma=False,
    )
```

```python
import functools

import jax
import jax.numpy as jnp
from jax import lax
from jax.experimental import pallas as pl
from jax.experimental.pallas import tpu as pltpu
from jax.sharding import PartitionSpec as P

CAP = 48
F32, BF16 = jnp.float32, jnp.bfloat16
MIB = 1024 * 1024

CHUNKS = ((3, "end"), (4, "end"), (4, "end"), (3, "end"), (2, "inner"))

ROUTES = {
    "end": {
        "m0": (0, 1, None), "m1": (1, 2, "m0"), "m2": (2, 3, "m1"),
        "a0": (3, 2, None), "a1": (2, 1, "a0"), "a2": (1, 0, "a1"),
    },
    "inner": {
        "m0": (0, 1, None), "mb": (3, 2, None), "m1": (1, 2, "m0"),
        "a0": (2, 1, None), "a1": (2, 3, None), "a2": (1, 0, "a0"),
    },
}
OWNER = {"end": (3, ("m2",)), "inner": (2, ("m1", "mb"))}
HELD = {"end": ("a2", "a1", "a0", None), "inner": ("a2", "a0", None, "a1")}

ORDER = (
    ("g", 0), ("m0", 0), ("g", 1), ("m0", 1), ("m1", 0), ("g", 2), ("m0", 2), ("m1", 1),
    ("m2", 0), ("g", 3), ("m0", 3), ("m1", 2), ("m2", 1), ("g", 4), ("m0", 4), ("m1", 3),
    ("h", 0), ("a0", 0), ("m2", 2), ("h", 1), ("a0", 1), ("m1", 4), ("mb", 4), ("m2", 3),
    ("a1", 0), ("a1", 1), ("h", 2), ("a0", 2), ("h", 4), ("a0", 4), ("a2", 0), ("a1", 4),
    ("h", 3), ("a0", 3), ("a2", 1), ("a1", 2), ("a2", 4), ("d", 0), ("a1", 3), ("a2", 2),
    ("d", 1), ("a2", 3), ("d", 4), ("d", 2), ("d", 3),
)

SMEM = pl.BlockSpec(memory_space=pltpu.SMEM)
VMEM = pl.BlockSpec(memory_space=pltpu.VMEM)
ANY = pl.BlockSpec(memory_space=pl.ANY)
HBM = pl.BlockSpec(memory_space=pltpu.HBM)


def call(kernel, name, outs, operands, specs, after, scratch=(), aliases=None, limit=42, cost=(0, 0)):
    count = len(operands)

    def body(*refs):
        kernel(*refs[:count], *refs[count + len(after) :])

    return pl.pallas_call(
        body,
        out_shape=outs,
        in_specs=list(specs) + [ANY] * len(after),
        out_specs=jax.tree.map(lambda _: VMEM, outs) if aliases is None else ANY,
        scratch_shapes=list(scratch),
        input_output_aliases=aliases or {},
        cost_estimate=pl.CostEstimate(flops=cost[0], bytes_accessed=cost[1], transcendentals=0),
        compiler_params=pltpu.CompilerParams(vmem_limit_bytes=limit * MIB),
        name=name,
    )(*operands, *after)


def chunk_widths(count):
    unit = 256 if count % 4096 == 0 else 128
    widths, start = [], 0
    for share, _ in CHUNKS:
        widths.append(max(unit, share * count // 16 // unit * unit))
    kept = []
    for width in widths:
        width = min(width, count - start)
        if width:
            kept.append(width)
        start += width
    kept[-1] += count - start
    return kept


def slot_hits(ids, group, local_count):
    tokens, lanes = ids.shape[1], local_count * CAP
    slot = lax.broadcasted_iota(jnp.int32, (lanes, tokens), 0)
    expert = jnp.full((lanes, tokens), group * local_count, jnp.int32)
    for step in range(1, local_count):
        passed = (slot >= CAP).astype(jnp.int32) if step == 1 else passed_next
        expert = expert + passed
        slot = slot - CAP * passed
        passed_next = (slot >= CAP).astype(jnp.int32)
    named = [ids[k : k + 1, :] == expert for k in range(ids.shape[0])]
    member = functools.reduce(jnp.logical_or, named)
    earlier = lax.broadcasted_iota(jnp.int32, (tokens, tokens), 0) < lax.broadcasted_iota(
        jnp.int32, (tokens, tokens), 1
    )
    position = jnp.dot(
        member.astype(F32).astype(BF16),
        earlier.astype(F32).astype(BF16),
        preferred_element_type=F32,
    )
    return member & (position.astype(jnp.int32) == slot), named


def pick(group, ids, tokens, local_count):
    def kernel(group_ref, ids_ref, tokens_ref, out_ref):
        hit, _ = slot_hits(ids_ref[...], group_ref[0], local_count)
        rows = jnp.dot(
            hit.astype(F32).astype(BF16), tokens_ref[...], preferred_element_type=F32
        ).astype(BF16)
        for e in range(local_count):
            out_ref[e] = rows[e * CAP : (e + 1) * CAP]

    shape = jax.ShapeDtypeStruct((local_count, CAP, tokens.shape[1]), BF16)
    return call(kernel, "pick", shape, [group, ids, tokens], [SMEM, VMEM, VMEM], [])


def gate_up(place, rows, weights, start, width, after):
    local_count, _, depth = rows[0].shape
    count = sum(part.shape[1] for part in rows)
    pieces = 3
    block = depth // pieces

    def kernel(place_ref, *refs):
        row_refs = refs[: len(rows)]
        weight_refs, full_ref, short_ref, held, sems = refs[len(rows) : len(rows) + 2], *refs[len(rows) + 2 :]
        copies = []
        for e in range(local_count):
            for i in range(2):
                for k in range(pieces):
                    at = (e * 2 + i) * pieces + k
                    copies.append(
                        pltpu.make_async_copy(
                            weight_refs[i].at[e, pl.ds(k * block, block), pl.ds(start, width)],
                            held.at[at],
                            sems.at[at],
                        )
                    )
        for copy in copies:
            copy.start()
        for e in range(local_count):
            x = jnp.concatenate([ref[e] for ref in row_refs], axis=0)
            for i in range(2):
                total = None
                for k in range(pieces):
                    at = (e * 2 + i) * pieces + k
                    copies[at].wait()
                    part = jnp.dot(
                        x[:, k * block : (k + 1) * block], held[at], preferred_element_type=F32
                    )
                    total = part if total is None else total + part
                full_ref[i, e] = total

                @pl.when(place_ref[0] == 0)
                def _():
                    short_ref[i, e] = total.astype(BF16)

    shape = (2, local_count, count, width)
    slots = 2 * local_count * pieces
    return call(
        kernel,
        "gate_up",
        [jax.ShapeDtypeStruct(shape, F32), jax.ShapeDtypeStruct(shape, BF16)],
        [place, *rows, *weights],
        [SMEM] + [VMEM] * len(rows) + [HBM, HBM],
        after,
        [pltpu.VMEM((slots, block, width), BF16), pltpu.SemaphoreType.DMA((slots,))],
        limit=42,
        cost=(4 * local_count * count * depth * width, 4 * local_count * depth * width),
    )


def add_to_send(place, at, full, got, after):
    def kernel(place_ref, full_ref, got_ref, out_ref):
        @pl.when(place_ref[0] == at)
        def _():
            for e in range(full_ref.shape[1]):
                for i in range(2):
                    out_ref[i, e] = (full_ref[i, e] + got_ref[i, e].astype(F32)).astype(BF16)

    shape = jax.ShapeDtypeStruct(full.shape, BF16)
    return call(kernel, "add_to_send", shape, [place, full, got], [SMEM, VMEM, VMEM], after)


def round_to_send(place, at, full, after):
    def kernel(place_ref, full_ref, out_ref):
        @pl.when(place_ref[0] == at)
        def _():
            out_ref[...] = full_ref[...].astype(BF16)

    shape = jax.ShapeDtypeStruct(full.shape, BF16)
    return call(kernel, "round_to_send", shape, [place, full], [SMEM, VMEM], after)


def hidden_values(place, at, full, got, after):
    def kernel(place_ref, full_ref, *refs):
        got_refs, out_ref = refs[:-1], refs[-1]

        @pl.when(place_ref[0] == at)
        def _():
            for e in range(full_ref.shape[1]):
                gate, up = full_ref[0, e], full_ref[1, e]
                for ref in got_refs:
                    gate, up = gate + ref[0, e].astype(F32), up + ref[1, e].astype(F32)
                out_ref[e] = (gate / (1.0 + jnp.exp(-gate)) * up).astype(BF16)

    shape = jax.ShapeDtypeStruct(full.shape[1:], BF16)
    return call(
        kernel, "hidden_values", shape, [place, full, *got], [SMEM] + [VMEM] * (1 + len(got)), after
    )


def pass_on(value, after):
    def kernel(value_ref, out_ref):
        del value_ref, out_ref

    shape = jax.ShapeDtypeStruct(value.shape, value.dtype)
    return call(kernel, "pass_on", shape, [value], [ANY], after, aliases={0: 0})


def down(place, held, down_weight, start, totals, row_counts, after):
    local_count, count, width = held[0].shape
    features = down_weight.shape[2]
    block = 256 if width % 256 == 0 else 128
    pieces = width // block
    places = len(held)

    def kernel(place_ref, *refs):
        held_refs, weight_ref = refs[:places], refs[places]
        total_refs = refs[places + 1 : places + 1 + len(totals)]
        out_refs = refs[places + 1 + len(totals) :][: len(row_counts)]
        hidden, weights, sems = refs[-3:]
        copies = []
        for e in range(local_count):
            for k in range(pieces):
                at = e * pieces + k
                copies.append(
                    pltpu.make_async_copy(
                        weight_ref.at[e, pl.ds(start + k * block, block), :],
                        weights.at[at],
                        sems.at[at],
                    )
                )
        for copy in copies:
            copy.start()
        for i in range(places):

            @pl.when(place_ref[0] == i)
            def _():
                hidden[...] = held_refs[i][...]

        for e in range(local_count):
            product = None
            for k in range(pieces):
                copies[e * pieces + k].wait()
                part = jnp.dot(
                    hidden[e, :, k * block : (k + 1) * block],
                    weights[e * pieces + k],
                    preferred_element_type=F32,
                )
                product = part if product is None else product + part
            first = 0
            for i, rows in enumerate(row_counts):
                value = product[first : first + rows]
                out_refs[i][e] = total_refs[i][e] + value if totals else value
                first += rows

    shapes = [jax.ShapeDtypeStruct((local_count, rows, features), F32) for rows in row_counts]
    operands = [place, *held, down_weight, *totals]
    return call(
        kernel,
        "down",
        shapes,
        operands,
        [SMEM] + [VMEM] * places + [HBM] + [VMEM] * len(totals),
        after,
        [
            pltpu.VMEM(held[0].shape, BF16),
            pltpu.VMEM((local_count * pieces, block, features), BF16),
            pltpu.SemaphoreType.DMA((local_count * pieces,)),
        ],
        limit=42,
        cost=(2 * local_count * count * features * width, 2 * local_count * features * width),
    )


def combine(group, ids, weights, sums, groups):
    local_count, _, features = sums[0].shape
    tokens = ids.shape[1]
    block = tokens // groups

    def kernel(group_ref, ids_ref, weights_ref, *refs):
        sum_refs, own_ref, sent = refs[: len(sums)], refs[len(sums)], refs[len(sums) + 1 :]
        hit, named = slot_hits(ids_ref[...], group_ref[0], local_count)
        scale = sum(
            jnp.where(named[k], weights_ref[k : k + 1, :], 0.0) for k in range(len(named))
        )
        scale = jnp.where(hit, scale, 0.0)
        scale_high = scale.astype(BF16)
        scale_low = (scale - scale_high.astype(F32)).astype(BF16)
        rows = jnp.concatenate(
            [functools.reduce(jnp.add, [ref[e] for ref in sum_refs]) for e in range(local_count)],
            axis=0,
        )
        rows_high = rows.astype(BF16)
        rows_low = (rows - rows_high.astype(F32)).astype(BF16)

        def product(a, b):
            return lax.dot_general(
                a, b, (((0,), (0,)), ((), ())), preferred_element_type=F32
            )

        mixed = (
            product(scale_high, rows_high)
            + product(scale_high, rows_low)
            + product(scale_low, rows_high)
        )
        for place in range(groups):
            piece = mixed[place * block : (place + 1) * block]
            step = group_ref[0] ^ place

            @pl.when(step == 0)
            def _():
                own_ref[...] = piece

            for other in range(1, groups):

                @pl.when(step == other)
                def _():
                    sent[other - 1][...] = piece.astype(BF16)

    return call(
        kernel,
        "combine",
        [jax.ShapeDtypeStruct((block, features), F32)]
        + [jax.ShapeDtypeStruct((block, features), BF16)] * (groups - 1),
        [group, ids, weights, *sums],
        [SMEM] + [VMEM] * (2 + len(sums)),
        [],
    )


def place_blocks(group, pieces):
    block, features = pieces[0].shape

    def kernel(group_ref, *refs):
        out_ref = refs[-1]
        for step, piece_ref in enumerate(refs[:-1]):
            start = pl.multiple_of((group_ref[0] ^ step) * block, block)
            out_ref[pl.ds(start, block), :] = piece_ref[...]

    shape = jax.ShapeDtypeStruct((block * len(pieces), features), BF16)
    return call(
        kernel, "place_blocks", shape, [group, *pieces], [SMEM] + [VMEM] * len(pieces), []
    )


def local(mesh_shape, tokens, expert_ids, route_weights, gate_weight, up_weight, down_weight):
    shards, groups, line = mesh_shape["dp"], mesh_shape["expert"], mesh_shape["blk"]
    local_count, _, hidden_count = gate_weight.shape
    group = lax.axis_index("expert").astype(jnp.int32).reshape(1)
    line_at = lax.axis_index("blk")
    odd = lax.axis_index("dp") % 2
    place = jnp.where(odd == 1, line - 1 - line_at, line_at).astype(jnp.int32).reshape(1)
    ids, choice_weights = expert_ids.T, route_weights.T
    swap = [(0, 1), (1, 0)]

    def hop(value, source, target):
        pairs = []
        for shard in range(shards):
            ends = (line - 1 - source, line - 1 - target) if shard % 2 else (source, target)
            pairs.append((shard * line + ends[0], shard * line + ends[1]))
        return lax.ppermute(value, ("dp", "blk"), pairs)

    rows = pick(group, ids, tokens, local_count)
    if shards == 2:
        rows = [rows, lax.ppermute(rows, "dp", swap)]
    else:
        rows = [lax.all_gather(rows, "dp", axis=1, tiled=True)]
    row_counts = [part.shape[1] for part in rows]

    widths = chunk_widths(hidden_count)
    starts = [sum(widths[:c]) for c in range(len(widths))]
    full, short, values, got, totals, after = {}, {}, {}, {}, [], []
    for name, c in ORDER:
        if c >= len(widths):
            continue
        kind = CHUNKS[c][1]
        route = ROUTES[kind]
        owner, summed_by = OWNER[kind]
        if name == "g":
            full[c], short[c] = gate_up(
                place, rows, (gate_weight, up_weight), starts[c], widths[c], after
            )
            after = [full[c]]
        elif name == "h":
            values[c] = hidden_values(place, owner, full[c], [got[c, m] for m in summed_by], after)
            after = [values[c]]
        elif name == "d":
            held = [values[c] if m is None else got[c, m] for m in HELD[kind]]
            totals = down(place, held, down_weight, starts[c], totals, row_counts, after)
            after = [totals[0]]
        else:
            source, target, needed = route[name]
            if name == "m0":
                sent = short[c]
            elif name == "mb":
                sent = round_to_send(place, source, full[c], after)
                after = [sent]
            elif name[0] == "m":
                sent = add_to_send(place, source, full[c], got[c, needed], after)
                after = [sent]
            elif needed is None:
                sent = values[c]
            else:
                sent = got[c, needed] = pass_on(got[c, needed], after)
                after = [sent]
            got[c, name] = hop(sent, source, target)

    if shards == 2:
        sums = [totals[0], lax.ppermute(totals[1], "dp", swap)]
    else:
        sums = [lax.psum_scatter(totals[0], "dp", scatter_dimension=1, tiled=True)]
    own, *sent = combine(group, ids, choice_weights, sums, groups)
    for step in range(groups - 1, 0, -1):
        exchange = [(i, i ^ step) for i in range(groups)]
        own = own + lax.ppermute(sent[step - 1], "expert", exchange).astype(F32)
    block = own.astype(BF16)
    pieces = [block]
    for step in range(1, groups):
        pieces.append(lax.ppermute(block, "expert", [(i, i ^ step) for i in range(groups)]))
    return place_blocks(group, pieces)


def solution(mesh):
    placed = (
        P("dp", "blk"),
        P("dp", None),
        P("dp", None),
        P("expert", "blk", "dp"),
        P("expert", "blk", "dp"),
        P("expert", "dp", "blk"),
    )
    return jax.shard_map(
        functools.partial(local, dict(mesh.shape)),
        mesh=mesh,
        in_specs=placed,
        out_specs=P("dp", "blk"),
        check_vma=False,
    )
```

```python
import functools

import jax
import jax.numpy as jnp
from jax import lax
from jax.experimental import pallas as pl
from jax.experimental.pallas import tpu as pltpu
from jax.sharding import PartitionSpec as P

CAP = 48
F32, BF16 = jnp.float32, jnp.bfloat16
MIB = 1024 * 1024

CHUNKS = ((3, "end"), (3, "end"), (3, "end"), (3, "inner"), (2, "inner"), (2, "inner"))

ROUTES = {
    "end": {
        "m0": (0, 1, None), "m1": (1, 2, "m0"), "m2": (2, 3, "m1"),
        "a0": (3, 2, None), "a1": (2, 1, "a0"), "a2": (1, 0, "a1"),
    },
    "inner": {
        "m0": (0, 1, None), "mb": (3, 2, None), "m1": (1, 2, "m0"),
        "a0": (2, 1, None), "a1": (2, 3, None), "a2": (2, 0, None),
    },
}
OWNER = {"end": (3, ("m2",)), "inner": (2, ("m1", "mb"))}
HELD = {"end": ("a2", "a1", "a0", None), "inner": ("a2", "a0", None, "a1")}

ORDER = (
    ("g", 0), ("m0", 0), ("g", 2), ("m0", 2), ("g", 1), ("m0", 1), ("m1", 0), ("g", 3),
    ("m0", 3), ("m1", 2), ("g", 4), ("m0", 4), ("m1", 1), ("m2", 0), ("mb", 3), ("m1", 3),
    ("m2", 2), ("mb", 4), ("g", 5), ("m0", 5), ("m2", 1), ("h", 0), ("m1", 4), ("h", 3),
    ("a0", 0), ("a0", 3), ("h", 2), ("a0", 2), ("m1", 5), ("mb", 5), ("a1", 0), ("h", 4),
    ("a1", 3), ("a2", 3), ("a2", 4), ("a1", 2), ("h", 1), ("a0", 1), ("h", 5), ("a1", 5),
    ("a1", 4), ("a2", 0), ("a1", 1), ("a2", 2), ("a2", 5), ("a0", 5), ("a0", 4), ("a2", 1),
    ("d", 3), ("d", 0), ("d", 5), ("d", 2), ("d", 4), ("d", 1),
)

SMEM = pl.BlockSpec(memory_space=pltpu.SMEM)
VMEM = pl.BlockSpec(memory_space=pltpu.VMEM)
ANY = pl.BlockSpec(memory_space=pl.ANY)
HBM = pl.BlockSpec(memory_space=pltpu.HBM)


def call(kernel, name, outs, operands, specs, after, scratch=(), aliases=None, limit=6):
    count = len(operands)

    def body(*refs):
        kernel(*refs[:count], *refs[count + len(after) :])

    return pl.pallas_call(
        body,
        out_shape=outs,
        in_specs=list(specs) + [ANY] * len(after),
        out_specs=jax.tree.map(lambda _: VMEM, outs) if aliases is None else ANY,
        scratch_shapes=list(scratch),
        input_output_aliases=aliases or {},
        compiler_params=pltpu.CompilerParams(vmem_limit_bytes=limit * MIB),
        name=name,
    )(*operands, *after)


def chunk_widths(count):
    unit = 256 if count % 4096 == 0 else 128
    widths, start = [], 0
    for share, _ in CHUNKS:
        widths.append(max(unit, share * count // 16 // unit * unit))
    kept = []
    for width in widths:
        width = min(width, count - start)
        if width:
            kept.append(width)
        start += width
    kept[-1] += count - start
    return kept


def slot_hits(ids, group, local_count):
    tokens, lanes = ids.shape[1], local_count * CAP
    slot = lax.broadcasted_iota(jnp.int32, (lanes, tokens), 0)
    expert = jnp.full((lanes, tokens), group * local_count, jnp.int32)
    for step in range(1, local_count):
        passed = (slot >= CAP).astype(jnp.int32) if step == 1 else passed_next
        expert = expert + passed
        slot = slot - CAP * passed
        passed_next = (slot >= CAP).astype(jnp.int32)
    named = [ids[k : k + 1, :] == expert for k in range(ids.shape[0])]
    member = functools.reduce(jnp.logical_or, named)
    earlier = lax.broadcasted_iota(jnp.int32, (tokens, tokens), 0) < lax.broadcasted_iota(
        jnp.int32, (tokens, tokens), 1
    )
    position = jnp.dot(
        member.astype(F32).astype(BF16),
        earlier.astype(F32).astype(BF16),
        preferred_element_type=F32,
    )
    return member & (position.astype(jnp.int32) == slot), named


def pick(group, ids, tokens, local_count):
    def kernel(group_ref, ids_ref, tokens_ref, out_ref):
        hit, _ = slot_hits(ids_ref[...], group_ref[0], local_count)
        rows = jnp.dot(
            hit.astype(F32).astype(BF16), tokens_ref[...], preferred_element_type=F32
        ).astype(BF16)
        for e in range(local_count):
            out_ref[e] = rows[e * CAP : (e + 1) * CAP]

    shape = jax.ShapeDtypeStruct((local_count, CAP, tokens.shape[1]), BF16)
    return call(kernel, "pick", shape, [group, ids, tokens], [SMEM, VMEM, VMEM], [])


def gate_up(place, rows, weights, start, width, after):
    local_count, _, depth = rows[0].shape
    count = sum(part.shape[1] for part in rows)
    pieces = 3
    block = depth // pieces

    def kernel(place_ref, *refs):
        row_refs = refs[: len(rows)]
        weight_refs, full_ref, short_ref, held, sems = refs[len(rows) : len(rows) + 2], *refs[len(rows) + 2 :]
        copies = []
        for e in range(local_count):
            for i in range(2):
                for k in range(pieces):
                    at = (e * 2 + i) * pieces + k
                    copies.append(
                        pltpu.make_async_copy(
                            weight_refs[i].at[e, pl.ds(k * block, block), pl.ds(start, width)],
                            held.at[at],
                            sems.at[at],
                        )
                    )
        for copy in copies:
            copy.start()
        for e in range(local_count):
            x = jnp.concatenate([ref[e] for ref in row_refs], axis=0)
            for i in range(2):
                total = None
                for k in range(pieces):
                    at = (e * 2 + i) * pieces + k
                    copies[at].wait()
                    part = jnp.dot(
                        x[:, k * block : (k + 1) * block], held[at], preferred_element_type=F32
                    )
                    total = part if total is None else total + part
                full_ref[i, e] = total

                @pl.when(place_ref[0] == 0)
                def _():
                    short_ref[i, e] = total.astype(BF16)

    shape = (2, local_count, count, width)
    slots = 2 * local_count * pieces
    return call(
        kernel,
        "gate_up",
        [jax.ShapeDtypeStruct(shape, F32), jax.ShapeDtypeStruct(shape, BF16)],
        [place, *rows, *weights],
        [SMEM] + [VMEM] * len(rows) + [HBM, HBM],
        after,
        [pltpu.VMEM((slots, block, width), BF16), pltpu.SemaphoreType.DMA((slots,))],
        limit=30,
    )


def add_to_send(place, at, full, got, after):
    def kernel(place_ref, full_ref, got_ref, out_ref):
        @pl.when(place_ref[0] == at)
        def _():
            for e in range(full_ref.shape[1]):
                for i in range(2):
                    out_ref[i, e] = (full_ref[i, e] + got_ref[i, e].astype(F32)).astype(BF16)

    shape = jax.ShapeDtypeStruct(full.shape, BF16)
    return call(kernel, "add_to_send", shape, [place, full, got], [SMEM, VMEM, VMEM], after)


def round_to_send(place, at, full, after):
    def kernel(place_ref, full_ref, out_ref):
        @pl.when(place_ref[0] == at)
        def _():
            out_ref[...] = full_ref[...].astype(BF16)

    shape = jax.ShapeDtypeStruct(full.shape, BF16)
    return call(kernel, "round_to_send", shape, [place, full], [SMEM, VMEM], after)


def hidden_values(place, at, full, got, after):
    def kernel(place_ref, full_ref, *refs):
        got_refs, out_ref = refs[:-1], refs[-1]

        @pl.when(place_ref[0] == at)
        def _():
            for e in range(full_ref.shape[1]):
                gate, up = full_ref[0, e], full_ref[1, e]
                for ref in got_refs:
                    gate, up = gate + ref[0, e].astype(F32), up + ref[1, e].astype(F32)
                out_ref[e] = (gate / (1.0 + jnp.exp(-gate)) * up).astype(BF16)

    shape = jax.ShapeDtypeStruct(full.shape[1:], BF16)
    return call(
        kernel, "hidden_values", shape, [place, full, *got], [SMEM] + [VMEM] * (1 + len(got)), after
    )


def pass_on(value, after):
    def kernel(value_ref, out_ref):
        del value_ref, out_ref

    shape = jax.ShapeDtypeStruct(value.shape, value.dtype)
    return call(kernel, "pass_on", shape, [value], [ANY], after, aliases={0: 0})


def down(place, held, down_weight, start, totals, row_counts, after):
    local_count, count, width = held[0].shape
    features = down_weight.shape[2]
    block = 256 if width % 256 == 0 else 128
    pieces = width // block
    places = len(held)

    def kernel(place_ref, *refs):
        held_refs, weight_ref = refs[:places], refs[places]
        total_refs = refs[places + 1 : places + 1 + len(totals)]
        out_refs = refs[places + 1 + len(totals) :][: len(row_counts)]
        hidden = refs[-1]
        for i in range(places):

            @pl.when(place_ref[0] == i)
            def _():
                hidden[...] = held_refs[i][...]

        for e in range(local_count):
            product = None
            for k in range(pieces):
                part = jnp.dot(
                    hidden[e, :, k * block : (k + 1) * block],
                    weight_ref[e, start + k * block : start + (k + 1) * block, :],
                    preferred_element_type=F32,
                )
                product = part if product is None else product + part
            first = 0
            for i, rows in enumerate(row_counts):
                value = product[first : first + rows]
                out_refs[i][e] = total_refs[i][e] + value if totals else value
                first += rows

    shapes = [jax.ShapeDtypeStruct((local_count, rows, features), F32) for rows in row_counts]
    operands = [place, *held, down_weight, *totals]
    return call(
        kernel,
        "down",
        shapes,
        operands,
        [SMEM] + [VMEM] * (places + 1 + len(totals)),
        after,
        [
            pltpu.VMEM(held[0].shape, BF16),
        ],
        limit=6 + 2 * local_count * count * features * 4 // MIB,
    )


def combine(group, ids, weights, sums):
    local_count, _, features = sums[0].shape
    tokens = ids.shape[1]

    def kernel(group_ref, ids_ref, weights_ref, *refs):
        sum_refs, out_ref = refs[:-1], refs[-1]
        hit, named = slot_hits(ids_ref[...], group_ref[0], local_count)
        scale = sum(
            jnp.where(named[k], weights_ref[k : k + 1, :], 0.0) for k in range(len(named))
        )
        scale = jnp.where(hit, scale, 0.0)
        scale_high = scale.astype(BF16)
        scale_low = (scale - scale_high.astype(F32)).astype(BF16)
        rows = jnp.concatenate(
            [functools.reduce(jnp.add, [ref[e] for ref in sum_refs]) for e in range(local_count)],
            axis=0,
        )
        rows_high = rows.astype(BF16)
        rows_low = (rows - rows_high.astype(F32)).astype(BF16)

        def product(a, b):
            return lax.dot_general(a, b, (((0,), (0,)), ((), ())), preferred_element_type=F32)

        mixed = (
            product(scale_high, rows_high)
            + product(scale_high, rows_low)
            + product(scale_low, rows_high)
        )
        out_ref[...] = mixed.astype(BF16)

    return call(
        kernel,
        "combine",
        jax.ShapeDtypeStruct((tokens, features), BF16),
        [group, ids, weights, *sums],
        [SMEM] + [VMEM] * (2 + len(sums)),
        [],
    )


def sum_blocks(parts):
    groups = parts.shape[0]

    def kernel(parts_ref, out_ref):
        total = parts_ref[0].astype(F32)
        for i in range(1, groups):
            total = total + parts_ref[i].astype(F32)
        total = total.astype(BF16)
        for i in range(groups):
            out_ref[i] = total

    shape = jax.ShapeDtypeStruct(parts.shape, BF16)
    return call(kernel, "sum_blocks", shape, [parts], [VMEM], [])


def local(mesh_shape, tokens, expert_ids, route_weights, gate_weight, up_weight, down_weight):
    shards, groups, line = mesh_shape["dp"], mesh_shape["expert"], mesh_shape["blk"]
    local_count, _, hidden_count = gate_weight.shape
    group = lax.axis_index("expert").astype(jnp.int32).reshape(1)
    line_at = lax.axis_index("blk")
    odd = lax.axis_index("dp") % 2
    place = jnp.where(odd == 1, line - 1 - line_at, line_at).astype(jnp.int32).reshape(1)
    ids, choice_weights = expert_ids.T, route_weights.T
    swap = [(0, 1), (1, 0)]

    def hop(value, source, target):
        pairs = []
        for shard in range(shards):
            ends = (line - 1 - source, line - 1 - target) if shard % 2 else (source, target)
            pairs.append((shard * line + ends[0], shard * line + ends[1]))
        return lax.ppermute(value, ("dp", "blk"), pairs)

    rows = pick(group, ids, tokens, local_count)
    if shards == 2:
        rows = [rows, lax.ppermute(rows, "dp", swap)]
    else:
        rows = [lax.all_gather(rows, "dp", axis=1, tiled=True)]
    row_counts = [part.shape[1] for part in rows]

    widths = chunk_widths(hidden_count)
    starts = [sum(widths[:c]) for c in range(len(widths))]
    full, short, values, got, totals, after = {}, {}, {}, {}, [], []
    for name, c in ORDER:
        if c >= len(widths):
            continue
        kind = CHUNKS[c][1]
        route = ROUTES[kind]
        owner, summed_by = OWNER[kind]
        if name == "g":
            full[c], short[c] = gate_up(
                place, rows, (gate_weight, up_weight), starts[c], widths[c], after
            )
            after = [full[c]]
        elif name == "h":
            values[c] = hidden_values(place, owner, full[c], [got[c, m] for m in summed_by], after)
            after = [values[c]]
        elif name == "d":
            held = [values[c] if m is None else got[c, m] for m in HELD[kind]]
            totals = down(place, held, down_weight, starts[c], totals, row_counts, after)
            after = [totals[0]]
        else:
            source, target, needed = route[name]
            if name == "m0":
                sent = short[c]
            elif name == "mb":
                sent = round_to_send(place, source, full[c], after)
                after = [sent]
            elif name[0] == "m":
                sent = add_to_send(place, source, full[c], got[c, needed], after)
                after = [sent]
            elif needed is None:
                sent = values[c]
            else:
                sent = got[c, needed] = pass_on(got[c, needed], after)
                after = [sent]
            got[c, name] = hop(sent, source, target)

    if shards == 2:
        sums = [totals[0], lax.ppermute(totals[1], "dp", swap)]
    else:
        sums = [lax.psum_scatter(totals[0], "dp", scatter_dimension=1, tiled=True)]
    mixed = combine(group, ids, choice_weights, sums)
    parts = mixed.reshape(groups, mixed.shape[0] // groups, mixed.shape[1])
    parts = lax.all_to_all(parts, "expert", 0, 0)
    return lax.all_to_all(sum_blocks(parts), "expert", 0, 0).reshape(mixed.shape)


def solution(mesh):
    placed = (
        P("dp", "blk"),
        P("dp", None),
        P("dp", None),
        P("expert", "blk", "dp"),
        P("expert", "blk", "dp"),
        P("expert", "dp", "blk"),
    )
    return jax.shard_map(
        functools.partial(local, dict(mesh.shape)),
        mesh=mesh,
        in_specs=placed,
        out_specs=P("dp", "blk"),
        check_vma=False,
    )
```

```python
import functools

import jax
import jax.numpy as jnp
from jax import lax
from jax.experimental import pallas as pl
from jax.experimental.pallas import tpu as pltpu
from jax.sharding import PartitionSpec as P

CAP = 48
F32, BF16 = jnp.float32, jnp.bfloat16
MIB = 1024 * 1024

SHARES = (2, 4, 4, 4, 2)
GROUPS = {0: (0, 1), 2: (2,), 3: (3,), 4: (4,)}

ORDER = (
    ("g", 1), ("h1", 1), ("g", 2), ("g", 0), ("h1", 0), ("h2", 1), ("h1", 2), ("g", 3),
    ("h2", 0), ("h1", 3), ("h3", 1), ("h2", 2), ("g", 4), ("h3", 0), ("h2", 3), ("h1", 4),
    ("h3", 2), ("s", 0), ("b1", 0), ("h3", 3), ("h2", 4), ("s", 2), ("b1", 2), ("b2", 0),
    ("h3", 4), ("s", 3), ("b1", 3), ("b2", 2), ("s", 4), ("b3", 0), ("b1", 4), ("b2", 3),
    ("b3", 2), ("b2", 4), ("b3", 3), ("d", 2), ("b3", 4), ("d", 0), ("d", 3), ("d", 4),
)

SMEM = pl.BlockSpec(memory_space=pltpu.SMEM)
VMEM = pl.BlockSpec(memory_space=pltpu.VMEM)
ANY = pl.BlockSpec(memory_space=pl.ANY)
HBM = pl.BlockSpec(memory_space=pltpu.HBM)


def call(kernel, name, outs, operands, specs, after, scratch=(), aliases=None, limit=6):
    count = len(operands)

    def body(*refs):
        kernel(*refs[:count], *refs[count + len(after) :])

    return pl.pallas_call(
        body,
        out_shape=outs,
        in_specs=list(specs) + [ANY] * len(after),
        out_specs=jax.tree.map(lambda _: VMEM, outs) if aliases is None else ANY,
        scratch_shapes=list(scratch),
        input_output_aliases=aliases or {},
        compiler_params=pltpu.CompilerParams(vmem_limit_bytes=limit * MIB),
        name=name,
    )(*operands, *after)


def chunk_widths(half):
    widths, start = [], 0
    for share in SHARES:
        width = min(max(128, share * half // 16 // 128 * 128), half - start)
        if width:
            widths.append(width)
        start += width
    widths[-1] += half - start
    return widths


def slot_hits(ids, group, local_count):
    tokens, lanes = ids.shape[1], local_count * CAP
    slot = lax.broadcasted_iota(jnp.int32, (lanes, tokens), 0)
    expert = jnp.full((lanes, tokens), group * local_count, jnp.int32)
    for step in range(1, local_count):
        passed = (slot >= CAP).astype(jnp.int32) if step == 1 else passed_next
        expert = expert + passed
        slot = slot - CAP * passed
        passed_next = (slot >= CAP).astype(jnp.int32)
    named = [ids[k : k + 1, :] == expert for k in range(ids.shape[0])]
    member = functools.reduce(jnp.logical_or, named)
    earlier = lax.broadcasted_iota(jnp.int32, (tokens, tokens), 0) < lax.broadcasted_iota(
        jnp.int32, (tokens, tokens), 1
    )
    position = jnp.dot(
        member.astype(F32).astype(BF16),
        earlier.astype(F32).astype(BF16),
        preferred_element_type=F32,
    )
    return member & (position.astype(jnp.int32) == slot), named


def pick(group, ids, tokens, local_count):
    def kernel(group_ref, ids_ref, tokens_ref, out_ref):
        hit, _ = slot_hits(ids_ref[...], group_ref[0], local_count)
        rows = jnp.dot(
            hit.astype(F32).astype(BF16), tokens_ref[...], preferred_element_type=F32
        ).astype(BF16)
        for e in range(local_count):
            out_ref[e] = rows[e * CAP : (e + 1) * CAP]

    shape = jax.ShapeDtypeStruct((local_count, CAP, tokens.shape[1]), BF16)
    return call(kernel, "pick", shape, [group, ids, tokens], [SMEM, VMEM, VMEM], [])


def gate_up(place, rows, weights, start, width, after):
    local_count, _, depth = rows[0].shape
    count = sum(part.shape[1] for part in rows)
    half = weights[0].shape[2] // 2
    pieces = 2
    block = depth // pieces

    def kernel(place_ref, *refs):
        row_refs, weight_refs = refs[: len(rows)], refs[len(rows) : len(rows) + 2]
        far_ref, short_ref, near_ref, held, sems = refs[len(rows) + 2 :]
        copies = {}
        for part in range(2):
            side = (1 - place_ref[1]) if part == 0 else place_ref[1]
            column = pl.multiple_of(side * half + start, 128)
            for e in range(local_count):
                for i in range(2):
                    at = (part * local_count + e) * 2 + i
                    for k in range(pieces):
                        copies[at, k] = pltpu.make_async_copy(
                            weight_refs[i].at[e, pl.ds(k * block, block), pl.ds(column, width)],
                            held.at[at, pl.ds(k * block, block), :],
                            sems.at[at * pieces + k],
                        )
                        copies[at, k].start()
        for part, full_ref in enumerate((far_ref, near_ref)):
            for e in range(local_count):
                x = jnp.concatenate([ref[e] for ref in row_refs], axis=0)
                for i in range(2):
                    at = (part * local_count + e) * 2 + i
                    for k in range(pieces):
                        copies[at, k].wait()
                    full_ref[i, e] = jnp.dot(x, held[at], preferred_element_type=F32)
                    if part == 0:

                        @pl.when(place_ref[0] == 1)
                        def _():
                            short_ref[i, e] = full_ref[i, e].astype(BF16)

    shape = (2, local_count, count, width)
    slots = 4 * local_count
    return call(
        kernel,
        "gate_up",
        [jax.ShapeDtypeStruct(shape, kind) for kind in (F32, BF16, F32)],
        [place, *rows, *weights],
        [SMEM] + [VMEM] * len(rows) + [HBM, HBM],
        after,
        [pltpu.VMEM((slots, depth, width), BF16), pltpu.SemaphoreType.DMA((slots * pieces,))],
        limit=30,
    )


def add_to_send(place, full, got, after):
    def kernel(place_ref, full_ref, got_ref, out_ref):
        @pl.when(place_ref[0] == 0)
        def _():
            for e in range(full_ref.shape[1]):
                for i in range(2):
                    out_ref[i, e] = (full_ref[i, e] + got_ref[i, e].astype(F32)).astype(BF16)

    shape = jax.ShapeDtypeStruct(full.shape, BF16)
    return call(kernel, "add_to_send", shape, [place, full, got], [SMEM, VMEM, VMEM], after)


def hidden_values(place, full, got, after):
    widths = [part.shape[3] for part in full]

    def kernel(place_ref, *refs):
        out_ref = refs[-1]

        @pl.when(place_ref[0] == 1)
        def _():
            start = 0
            for c, width in enumerate(widths):
                full_ref, got_ref = refs[c], refs[len(widths) + c]
                for e in range(out_ref.shape[0]):
                    gate = full_ref[0, e] + got_ref[0, e].astype(F32)
                    up = full_ref[1, e] + got_ref[1, e].astype(F32)
                    value = gate / (1.0 + jnp.exp(-gate)) * up
                    out_ref[e, :, start : start + width] = value.astype(BF16)
                start += width

    shape = jax.ShapeDtypeStruct(full[0].shape[1:3] + (sum(widths),), BF16)
    specs = [SMEM] + [VMEM] * (2 * len(widths))
    return call(kernel, "hidden_values", shape, [place, *full, *got], specs, after)


def pass_on(value, after):
    def kernel(value_ref, out_ref):
        del value_ref, out_ref

    shape = jax.ShapeDtypeStruct(value.shape, value.dtype)
    return call(kernel, "pass_on", shape, [value], [ANY], after, aliases={0: 0})


def down(place, held, down_weight, starts, widths, totals, row_counts, after):
    local_count, count, width = held[0].shape
    features = down_weight.shape[2]
    half = down_weight.shape[1] // 2

    def kernel(place_ref, *refs):
        held_refs, weight_ref = refs[:4], refs[4]
        total_refs = refs[5 : 5 + len(totals)]
        out_refs, hidden = refs[5 + len(totals) : -1], refs[-1]
        for part in range(2):
            for kind in range(2):

                @pl.when(place_ref[0] == 1 - kind)
                def _():
                    hidden[part] = held_refs[part * 2 + kind][...]

        for e in range(local_count):
            product = None
            for part in range(2):
                side = place_ref[1] if part == 0 else (1 - place_ref[1])
                column = 0
                for start, size in zip(starts, widths):
                    row = pl.multiple_of(side * half + start, 128)
                    value = jnp.dot(
                        hidden[part, e, :, column : column + size],
                        weight_ref[e, pl.ds(row, size), :],
                        preferred_element_type=F32,
                    )
                    product = value if product is None else product + value
                    column += size
            first = 0
            for i, rows in enumerate(row_counts):
                value = product[first : first + rows]
                out_refs[i][e] = total_refs[i][e] + value if totals else value
                first += rows

    return call(
        kernel,
        "down",
        [jax.ShapeDtypeStruct((local_count, rows, features), F32) for rows in row_counts],
        [place, *held, down_weight, *totals],
        [SMEM] + [VMEM] * (5 + len(totals)),
        after,
        [pltpu.VMEM((2,) + held[0].shape, BF16)],
        limit=6 + 2 * local_count * count * features * 4 // MIB,
    )


def combine(group, ids, weights, sums, groups):
    local_count, _, features = sums[0].shape
    tokens = ids.shape[1]
    block = tokens // groups

    def kernel(group_ref, ids_ref, weights_ref, *refs):
        sum_refs, own_ref, sent = refs[: len(sums)], refs[len(sums)], refs[len(sums) + 1 :]
        hit, named = slot_hits(ids_ref[...], group_ref[0], local_count)
        scale = sum(
            jnp.where(named[k], weights_ref[k : k + 1, :], 0.0) for k in range(len(named))
        )
        scale = jnp.where(hit, scale, 0.0)
        scale_high = scale.astype(BF16)
        scale_low = (scale - scale_high.astype(F32)).astype(BF16)
        rows = jnp.concatenate(
            [functools.reduce(jnp.add, [ref[e] for ref in sum_refs]) for e in range(local_count)],
            axis=0,
        )
        rows_high = rows.astype(BF16)
        rows_low = (rows - rows_high.astype(F32)).astype(BF16)

        def product(a, b):
            return lax.dot_general(
                a, b, (((0,), (0,)), ((), ())), preferred_element_type=F32
            )

        mixed = (
            product(scale_high, rows_high)
            + product(scale_high, rows_low)
            + product(scale_low, rows_high)
        )
        for place in range(groups):
            piece = mixed[place * block : (place + 1) * block]
            step = group_ref[0] ^ place

            @pl.when(step == 0)
            def _():
                own_ref[...] = piece

            for other in range(1, groups):

                @pl.when(step == other)
                def _():
                    sent[other - 1][...] = piece.astype(BF16)

    return call(
        kernel,
        "combine",
        [jax.ShapeDtypeStruct((block, features), F32)]
        + [jax.ShapeDtypeStruct((block, features), BF16)] * (groups - 1),
        [group, ids, weights, *sums],
        [SMEM] + [VMEM] * (2 + len(sums)),
        [],
    )


def place_blocks(group, pieces):
    block, features = pieces[0].shape

    def kernel(group_ref, *refs):
        out_ref = refs[-1]
        for step, piece_ref in enumerate(refs[:-1]):
            start = pl.multiple_of((group_ref[0] ^ step) * block, block)
            out_ref[pl.ds(start, block), :] = piece_ref[...]

    shape = jax.ShapeDtypeStruct((block * len(pieces), features), BF16)
    return call(
        kernel, "place_blocks", shape, [group, *pieces], [SMEM] + [VMEM] * len(pieces), []
    )


def local(mesh_shape, tokens, expert_ids, route_weights, gate_weight, up_weight, down_weight):
    shards, groups, line = mesh_shape["dp"], mesh_shape["expert"], mesh_shape["blk"]
    local_count, _, hidden_count = gate_weight.shape
    group = lax.axis_index("expert").astype(jnp.int32).reshape(1)
    line_at = lax.axis_index("blk")
    at_end = (line_at == 0) | (line_at == line - 1)
    near = line_at >= line // 2
    place = jnp.stack([at_end, near]).astype(jnp.int32)
    ids, choice_weights = expert_ids.T, route_weights.T
    swap = [(0, 1), (1, 0)]
    hops = {"1": [(0, 1), (3, 2)], "2": [(0, 0), (1, 2), (2, 1), (3, 3)], "3": [(1, 0), (2, 3)]}

    rows = pick(group, ids, tokens, local_count)
    if shards == 2:
        rows = [rows, lax.ppermute(rows, "dp", swap)]
    else:
        rows = [lax.all_gather(rows, "dp", axis=1, tiled=True)]
    row_counts = [part.shape[1] for part in rows]

    widths = chunk_widths(hidden_count // 2)
    starts = [sum(widths[:c]) for c in range(len(widths))]
    far, short, near_part, values, got, totals, after = {}, {}, {}, {}, {}, [], []
    for name, c in ORDER:
        if c >= len(widths):
            continue
        group_of = [q for q in GROUPS.get(c, ()) if q < len(widths)]
        if name == "g":
            far[c], short[c], near_part[c] = gate_up(
                place, rows, (gate_weight, up_weight), starts[c], widths[c], after
            )
            after = [far[c]]
        elif name == "s":
            values[c] = hidden_values(
                place, [near_part[q] for q in group_of], [got["h3", q] for q in group_of], after
            )
            after = [values[c]]
        elif name == "d":
            totals = down(
                place,
                [values[c], got["b1", c], got["b3", c], got["b2", c]],
                down_weight,
                [starts[q] for q in group_of],
                [widths[q] for q in group_of],
                totals,
                row_counts,
                after,
            )
            after = [totals[0]]
        else:
            if name == "h1":
                sent = short[c]
            elif name == "b1":
                sent = values[c]
            else:
                before = (name[0] + str(int(name[1]) - 1), c)
                if name[0] == "h":
                    full = far[c] if name == "h2" else near_part[c]
                    sent = add_to_send(place, full, got[before], after)
                else:
                    sent = got[before] = pass_on(got[before], after)
                after = [sent]
            got[name, c] = lax.ppermute(sent, "blk", hops[name[1]])

    if shards == 2:
        sums = [totals[0], lax.ppermute(totals[1], "dp", swap)]
    else:
        sums = [lax.psum_scatter(totals[0], "dp", scatter_dimension=1, tiled=True)]
    own, *sent = combine(group, ids, choice_weights, sums, groups)
    for step in range(groups - 1, 0, -1):
        exchange = [(i, i ^ step) for i in range(groups)]
        own = own + lax.ppermute(sent[step - 1], "expert", exchange).astype(F32)
    block = own.astype(BF16)
    pieces = [block]
    for step in range(1, groups):
        pieces.append(lax.ppermute(block, "expert", [(i, i ^ step) for i in range(groups)]))
    return place_blocks(group, pieces)


def solution(mesh):
    placed = (
        P("dp", "blk"),
        P("dp", None),
        P("dp", None),
        P("expert", "blk", "dp"),
        P("expert", "blk", "dp"),
        P("expert", "dp", "blk"),
    )
    return jax.shard_map(
        functools.partial(local, dict(mesh.shape)),
        mesh=mesh,
        in_specs=placed,
        out_specs=P("dp", "blk"),
        check_vma=False,
    )
```

```python
import functools

import jax
import jax.numpy as jnp
from jax import lax
from jax.experimental import pallas as pl
from jax.experimental.pallas import tpu as pltpu
from jax.sharding import PartitionSpec as P

CAP = 48
F32, BF16 = jnp.float32, jnp.bfloat16
MIB = 1024 * 1024

CHUNKS = ((2, "end"), (4, "end"), (4, "end"), (4, "inner"), (2, "direct"))

ROUTES = {
    "end": {
        "m0": (0, 1, None), "m1": (1, 2, "m0"), "m2": (2, 3, "m1"),
        "a0": (3, 2, None), "a1": (2, 1, "a0"), "a2": (1, 0, "a1"),
    },
    "inner": {
        "m0": (0, 1, None), "mb": (3, 2, None), "m1": (1, 2, "m0"),
        "a0": (2, 1, None), "a1": (2, 3, None), "a2": (1, 0, "a0"),
    },
    "direct": {
        "m0": (0, 1, None), "mb": (3, 2, None), "m1": (1, 2, "m0"),
        "a0": (2, 1, None), "a1": (2, 3, None), "a2": (2, 0, None),
    },
}
OWNER = {"end": (3, ("m2",)), "inner": (2, ("m1", "mb")), "direct": (2, ("m1", "mb"))}
HELD = {
    "end": ("a2", "a1", "a0", None),
    "inner": ("a2", "a0", None, "a1"),
    "direct": ("a2", "a0", None, "a1"),
}

ORDER = (
    ("g", 0), ("m0", 0), ("g", 2), ("m0", 2), ("m1", 0), ("g", 1), ("m2", 0), ("h", 0),
    ("m0", 1), ("m1", 2), ("a0", 0), ("g", 3), ("m0", 3), ("m1", 1), ("m2", 2), ("mb", 3),
    ("a1", 0), ("g", 4), ("m1", 3), ("a2", 0), ("h", 2), ("m0", 4), ("m2", 1), ("d", 0),
    ("m1", 4), ("a0", 2), ("h", 3), ("a0", 3), ("a1", 3), ("h", 1), ("a0", 1), ("a1", 2),
    ("a2", 3), ("a1", 1), ("a2", 2), ("d", 3), ("mb", 4), ("a2", 1), ("h", 4), ("a0", 4),
    ("a2", 4), ("a1", 4), ("d", 2), ("d", 1), ("d", 4),
)

SMEM = pl.BlockSpec(memory_space=pltpu.SMEM)
VMEM = pl.BlockSpec(memory_space=pltpu.VMEM)
ANY = pl.BlockSpec(memory_space=pl.ANY)
HBM = pl.BlockSpec(memory_space=pltpu.HBM)


def call(kernel, name, outs, operands, specs, after, scratch=(), aliases=None, limit=6):
    count = len(operands)

    def body(*refs):
        kernel(*refs[:count], *refs[count + len(after) :])

    return pl.pallas_call(
        body,
        out_shape=outs,
        in_specs=list(specs) + [ANY] * len(after),
        out_specs=jax.tree.map(lambda _: VMEM, outs) if aliases is None else ANY,
        scratch_shapes=list(scratch),
        input_output_aliases=aliases or {},
        compiler_params=pltpu.CompilerParams(vmem_limit_bytes=limit * MIB),
        name=name,
    )(*operands, *after)


def chunk_widths(count):
    unit = 256 if count % 4096 == 0 else 128
    widths, start = [], 0
    for share, _ in CHUNKS:
        widths.append(max(unit, share * count // 16 // unit * unit))
    kept = []
    for width in widths:
        width = min(width, count - start)
        if width:
            kept.append(width)
        start += width
    kept[-1] += count - start
    return kept


def slot_hits(ids, group, local_count):
    tokens, lanes = ids.shape[1], local_count * CAP
    slot = lax.broadcasted_iota(jnp.int32, (lanes, tokens), 0)
    expert = jnp.full((lanes, tokens), group * local_count, jnp.int32)
    for step in range(1, local_count):
        passed = (slot >= CAP).astype(jnp.int32) if step == 1 else passed_next
        expert = expert + passed
        slot = slot - CAP * passed
        passed_next = (slot >= CAP).astype(jnp.int32)
    named = [ids[k : k + 1, :] == expert for k in range(ids.shape[0])]
    member = functools.reduce(jnp.logical_or, named)
    earlier = lax.broadcasted_iota(jnp.int32, (tokens, tokens), 0) < lax.broadcasted_iota(
        jnp.int32, (tokens, tokens), 1
    )
    position = jnp.dot(
        member.astype(F32).astype(BF16),
        earlier.astype(F32).astype(BF16),
        preferred_element_type=F32,
    )
    return member & (position.astype(jnp.int32) == slot), named


def pick(group, ids, tokens, local_count):
    def kernel(group_ref, ids_ref, tokens_ref, out_ref):
        hit, _ = slot_hits(ids_ref[...], group_ref[0], local_count)
        rows = jnp.dot(
            hit.astype(F32).astype(BF16), tokens_ref[...], preferred_element_type=F32
        ).astype(BF16)
        for e in range(local_count):
            out_ref[e] = rows[e * CAP : (e + 1) * CAP]

    shape = jax.ShapeDtypeStruct((local_count, CAP, tokens.shape[1]), BF16)
    return call(kernel, "pick", shape, [group, ids, tokens], [SMEM, VMEM, VMEM], [])


def gate_up(place, rows, weights, start, width, after):
    local_count, _, depth = rows[0].shape
    count = sum(part.shape[1] for part in rows)
    pieces = 3
    block = depth // pieces

    def kernel(place_ref, *refs):
        row_refs, weight_refs = refs[: len(rows)], refs[len(rows) : len(rows) + 2]
        full_ref, short_ref, held, sems = refs[len(rows) + 2 :]
        copies = {}
        for at in range(2 * local_count):
            for k in range(pieces):
                copies[at, k] = pltpu.make_async_copy(
                    weight_refs[at % 2].at[at // 2, pl.ds(k * block, block), pl.ds(start, width)],
                    held.at[at, pl.ds(k * block, block), :],
                    sems.at[at * pieces + k],
                )
                copies[at, k].start()
        for e in range(local_count):
            x = jnp.concatenate([ref[e] for ref in row_refs], axis=0)
            for i in range(2):
                at = e * 2 + i
                for k in range(pieces):
                    copies[at, k].wait()
                full_ref[i, e] = jnp.dot(x, held[at], preferred_element_type=F32)

                @pl.when(place_ref[0] == 0)
                def _():
                    short_ref[i, e] = full_ref[i, e].astype(BF16)

    shape = (2, local_count, count, width)
    slots = 2 * local_count
    return call(
        kernel,
        "gate_up",
        [jax.ShapeDtypeStruct(shape, F32), jax.ShapeDtypeStruct(shape, BF16)],
        [place, *rows, *weights],
        [SMEM] + [VMEM] * len(rows) + [HBM, HBM],
        after,
        [pltpu.VMEM((slots, depth, width), BF16), pltpu.SemaphoreType.DMA((slots * pieces,))],
        limit=30,
    )


def add_to_send(place, at, full, got, after):
    def kernel(place_ref, full_ref, got_ref, out_ref):
        @pl.when(place_ref[0] == at)
        def _():
            for e in range(full_ref.shape[1]):
                for i in range(2):
                    out_ref[i, e] = (full_ref[i, e] + got_ref[i, e].astype(F32)).astype(BF16)

    shape = jax.ShapeDtypeStruct(full.shape, BF16)
    return call(kernel, "add_to_send", shape, [place, full, got], [SMEM, VMEM, VMEM], after)


def round_to_send(place, at, full, after):
    def kernel(place_ref, full_ref, out_ref):
        @pl.when(place_ref[0] == at)
        def _():
            out_ref[...] = full_ref[...].astype(BF16)

    shape = jax.ShapeDtypeStruct(full.shape, BF16)
    return call(kernel, "round_to_send", shape, [place, full], [SMEM, VMEM], after)


def hidden_values(place, at, full, got, after):
    def kernel(place_ref, full_ref, *refs):
        got_refs, out_ref = refs[:-1], refs[-1]

        @pl.when(place_ref[0] == at)
        def _():
            for e in range(full_ref.shape[1]):
                gate, up = full_ref[0, e], full_ref[1, e]
                for ref in got_refs:
                    gate, up = gate + ref[0, e].astype(F32), up + ref[1, e].astype(F32)
                out_ref[e] = (gate / (1.0 + jnp.exp(-gate)) * up).astype(BF16)

    shape = jax.ShapeDtypeStruct(full.shape[1:], BF16)
    return call(
        kernel, "hidden_values", shape, [place, full, *got], [SMEM] + [VMEM] * (1 + len(got)), after
    )


def pass_on(value, after):
    def kernel(value_ref, out_ref):
        del value_ref, out_ref

    shape = jax.ShapeDtypeStruct(value.shape, value.dtype)
    return call(kernel, "pass_on", shape, [value], [ANY], after, aliases={0: 0})


def down(place, held, down_weight, start, totals, row_counts, after):
    local_count, count, width = held[0].shape
    features = down_weight.shape[2]
    block = 256 if width % 256 == 0 else 128
    pieces = width // block
    places = len(held)

    def kernel(place_ref, *refs):
        held_refs, weight_ref = refs[:places], refs[places]
        total_refs = refs[places + 1 : places + 1 + len(totals)]
        out_refs = refs[places + 1 + len(totals) :][: len(row_counts)]
        hidden = refs[-1]
        for i in range(places):

            @pl.when(place_ref[0] == i)
            def _():
                hidden[...] = held_refs[i][...]

        for e in range(local_count):
            product = None
            for k in range(pieces):
                part = jnp.dot(
                    hidden[e, :, k * block : (k + 1) * block],
                    weight_ref[e, start + k * block : start + (k + 1) * block, :],
                    preferred_element_type=F32,
                )
                product = part if product is None else product + part
            first = 0
            for i, rows in enumerate(row_counts):
                value = product[first : first + rows]
                out_refs[i][e] = total_refs[i][e] + value if totals else value
                first += rows

    shapes = [jax.ShapeDtypeStruct((local_count, rows, features), F32) for rows in row_counts]
    operands = [place, *held, down_weight, *totals]
    return call(
        kernel,
        "down",
        shapes,
        operands,
        [SMEM] + [VMEM] * (places + 1 + len(totals)),
        after,
        [
            pltpu.VMEM(held[0].shape, BF16),
        ],
        limit=6 + 2 * local_count * count * features * 4 // MIB,
    )


def combine(group, ids, weights, sums, groups):
    local_count, _, features = sums[0].shape
    tokens = ids.shape[1]
    block = tokens // groups

    def kernel(group_ref, ids_ref, weights_ref, *refs):
        sum_refs, own_ref, sent = refs[: len(sums)], refs[len(sums)], refs[len(sums) + 1 :]
        hit, named = slot_hits(ids_ref[...], group_ref[0], local_count)
        scale = sum(
            jnp.where(named[k], weights_ref[k : k + 1, :], 0.0) for k in range(len(named))
        )
        scale = jnp.where(hit, scale, 0.0)
        scale_high = scale.astype(BF16)
        scale_low = (scale - scale_high.astype(F32)).astype(BF16)
        rows = jnp.concatenate(
            [functools.reduce(jnp.add, [ref[e] for ref in sum_refs]) for e in range(local_count)],
            axis=0,
        )
        rows_high = rows.astype(BF16)
        rows_low = (rows - rows_high.astype(F32)).astype(BF16)

        def product(a, b):
            return lax.dot_general(
                a, b, (((0,), (0,)), ((), ())), preferred_element_type=F32
            )

        mixed = (
            product(scale_high, rows_high)
            + product(scale_high, rows_low)
            + product(scale_low, rows_high)
        )
        for place in range(groups):
            piece = mixed[place * block : (place + 1) * block]
            step = group_ref[0] ^ place

            @pl.when(step == 0)
            def _():
                own_ref[...] = piece

            for other in range(1, groups):

                @pl.when(step == other)
                def _():
                    sent[other - 1][...] = piece.astype(BF16)

    return call(
        kernel,
        "combine",
        [jax.ShapeDtypeStruct((block, features), F32)]
        + [jax.ShapeDtypeStruct((block, features), BF16)] * (groups - 1),
        [group, ids, weights, *sums],
        [SMEM] + [VMEM] * (2 + len(sums)),
        [],
    )


def place_blocks(group, pieces):
    block, features = pieces[0].shape

    def kernel(group_ref, *refs):
        out_ref = refs[-1]
        for step, piece_ref in enumerate(refs[:-1]):
            start = pl.multiple_of((group_ref[0] ^ step) * block, block)
            out_ref[pl.ds(start, block), :] = piece_ref[...]

    shape = jax.ShapeDtypeStruct((block * len(pieces), features), BF16)
    return call(
        kernel, "place_blocks", shape, [group, *pieces], [SMEM] + [VMEM] * len(pieces), []
    )


def local(mesh_shape, tokens, expert_ids, route_weights, gate_weight, up_weight, down_weight):
    shards, groups, line = mesh_shape["dp"], mesh_shape["expert"], mesh_shape["blk"]
    local_count, _, hidden_count = gate_weight.shape
    group = lax.axis_index("expert").astype(jnp.int32).reshape(1)
    line_at = lax.axis_index("blk")
    odd = lax.axis_index("dp") % 2
    place = jnp.where(odd == 1, line - 1 - line_at, line_at).astype(jnp.int32).reshape(1)
    ids, choice_weights = expert_ids.T, route_weights.T
    swap = [(0, 1), (1, 0)]

    def hop(value, source, target):
        pairs = []
        for shard in range(shards):
            ends = (line - 1 - source, line - 1 - target) if shard % 2 else (source, target)
            pairs.append((shard * line + ends[0], shard * line + ends[1]))
        return lax.ppermute(value, ("dp", "blk"), pairs)

    rows = pick(group, ids, tokens, local_count)
    if shards == 2:
        rows = [rows, lax.ppermute(rows, "dp", swap)]
    else:
        rows = [lax.all_gather(rows, "dp", axis=1, tiled=True)]
    row_counts = [part.shape[1] for part in rows]

    widths = chunk_widths(hidden_count)
    starts = [sum(widths[:c]) for c in range(len(widths))]
    full, short, values, got, totals, after = {}, {}, {}, {}, [], []
    for name, c in ORDER:
        if c >= len(widths):
            continue
        kind = CHUNKS[c][1]
        route = ROUTES[kind]
        owner, summed_by = OWNER[kind]
        if name == "g":
            full[c], short[c] = gate_up(
                place, rows, (gate_weight, up_weight), starts[c], widths[c], after
            )
            after = [full[c]]
        elif name == "h":
            values[c] = hidden_values(place, owner, full[c], [got[c, m] for m in summed_by], after)
            after = [values[c]]
        elif name == "d":
            held = [values[c] if m is None else got[c, m] for m in HELD[kind]]
            totals = down(place, held, down_weight, starts[c], totals, row_counts, after)
            after = [totals[0]]
        else:
            source, target, needed = route[name]
            if name == "m0":
                sent = short[c]
            elif name == "mb":
                sent = round_to_send(place, source, full[c], after)
                after = [sent]
            elif name[0] == "m":
                sent = add_to_send(place, source, full[c], got[c, needed], after)
                after = [sent]
            elif needed is None:
                sent = values[c]
            else:
                sent = got[c, needed] = pass_on(got[c, needed], after)
                after = [sent]
            got[c, name] = hop(sent, source, target)

    if shards == 2:
        sums = [totals[0], lax.ppermute(totals[1], "dp", swap)]
    else:
        sums = [lax.psum_scatter(totals[0], "dp", scatter_dimension=1, tiled=True)]
    own, *sent = combine(group, ids, choice_weights, sums, groups)
    for step in range(groups - 1, 0, -1):
        exchange = [(i, i ^ step) for i in range(groups)]
        own = own + lax.ppermute(sent[step - 1], "expert", exchange).astype(F32)
    block = own.astype(BF16)
    pieces = [block]
    for step in range(1, groups):
        pieces.append(lax.ppermute(block, "expert", [(i, i ^ step) for i in range(groups)]))
    return place_blocks(group, pieces)


def solution(mesh):
    placed = (
        P("dp", "blk"),
        P("dp", None),
        P("dp", None),
        P("expert", "blk", "dp"),
        P("expert", "blk", "dp"),
        P("expert", "dp", "blk"),
    )
    return jax.shard_map(
        functools.partial(local, dict(mesh.shape)),
        mesh=mesh,
        in_specs=placed,
        out_specs=P("dp", "blk"),
        check_vma=False,
    )
```

```python
import functools

import jax
import jax.numpy as jnp
from jax import lax
from jax.experimental import pallas as pl
from jax.experimental.pallas import tpu as pltpu
from jax.sharding import PartitionSpec as P

CAP = 48
F32, BF16 = jnp.float32, jnp.bfloat16
MIB = 1024 * 1024

CHUNKS = ((3, "end"), (3, "end"), (3, "end"), (3, "end"), (2, "inner"), (2, "inner"))
GROUPS = {0: ((0,), "relay"), 1: ((1,), "relay"), 2: ((2,), "relay"), 3: ((3,), "relay"), 4: ((4,), "relay"), 5: ((5,), "relay")}

SUMS = {
    "end": {"m0": (0, 1, None), "m1": (1, 2, "m0"), "m2": (2, 3, "m1")},
    "inner": {"m0": (0, 1, None), "mb": (3, 2, None), "m1": (1, 2, "m0")},
}
BACK = {
    ("end", "relay"): {"a0": (3, 2, None), "a1": (2, 1, "a0"), "a2": (1, 0, "a1")},
    ("end", "direct"): {"a0": (3, 2, None), "a1": (3, 1, None), "a2": (3, 0, None)},
    ("inner", "relay"): {"a0": (2, 1, None), "a1": (2, 3, None), "a2": (1, 0, "a0")},
    ("inner", "direct"): {"a0": (2, 1, None), "a1": (2, 3, None), "a2": (2, 0, None)},
}
OWNER = {"end": (3, ("m2",)), "inner": (2, ("m1", "mb"))}
HELD = {"end": ("a2", "a1", "a0", None), "inner": ("a2", "a0", None, "a1")}

ORDER = (
    ("g", 0), ("m0", 0), ("g", 4), ("m0", 4), ("g", 2), ("m0", 2), ("m1", 0), ("g", 1),
    ("m0", 1), ("g", 3), ("m0", 3), ("m1", 2), ("mb", 4), ("m2", 0), ("g", 5), ("m0", 5),
    ("m1", 1), ("m2", 2), ("h", 0), ("a0", 0), ("m1", 3), ("m1", 4), ("m2", 1), ("h", 2),
    ("a1", 0), ("m2", 3), ("a0", 2), ("m1", 5), ("a1", 2), ("a2", 0), ("h", 1), ("h", 4),
    ("a2", 2), ("a0", 4), ("a0", 1), ("a1", 1), ("a2", 4), ("h", 3), ("d", 0), ("a1", 4),
    ("mb", 5), ("a2", 1), ("d", 2), ("a0", 3), ("a1", 3), ("d", 1), ("h", 5), ("a2", 3),
    ("d", 4), ("a0", 5), ("a1", 5), ("a2", 5), ("d", 3), ("d", 5),
)

SMEM = pl.BlockSpec(memory_space=pltpu.SMEM)
VMEM = pl.BlockSpec(memory_space=pltpu.VMEM)
ANY = pl.BlockSpec(memory_space=pl.ANY)
HBM = pl.BlockSpec(memory_space=pltpu.HBM)


def call(kernel, name, outs, operands, specs, after, scratch=(), aliases=None, limit=6):
    count = len(operands)

    def body(*refs):
        kernel(*refs[:count], *refs[count + len(after) :])

    return pl.pallas_call(
        body,
        out_shape=outs,
        in_specs=list(specs) + [ANY] * len(after),
        out_specs=jax.tree.map(lambda _: VMEM, outs) if aliases is None else ANY,
        scratch_shapes=list(scratch),
        input_output_aliases=aliases or {},
        compiler_params=pltpu.CompilerParams(vmem_limit_bytes=limit * MIB),
        name=name,
    )(*operands, *after)


def chunk_widths(count):
    unit = 256 if count % 4096 == 0 else 128
    widths, start = [], 0
    for share, _ in CHUNKS:
        widths.append(max(unit, share * count // 16 // unit * unit))
    kept = []
    for width in widths:
        width = min(width, count - start)
        if width:
            kept.append(width)
        start += width
    kept[-1] += count - start
    return kept


def slot_hits(ids, group, local_count):
    tokens, lanes = ids.shape[1], local_count * CAP
    slot = lax.broadcasted_iota(jnp.int32, (lanes, tokens), 0)
    expert = jnp.full((lanes, tokens), group * local_count, jnp.int32)
    for step in range(1, local_count):
        passed = (slot >= CAP).astype(jnp.int32) if step == 1 else passed_next
        expert = expert + passed
        slot = slot - CAP * passed
        passed_next = (slot >= CAP).astype(jnp.int32)
    named = [ids[k : k + 1, :] == expert for k in range(ids.shape[0])]
    member = functools.reduce(jnp.logical_or, named)
    earlier = lax.broadcasted_iota(jnp.int32, (tokens, tokens), 0) < lax.broadcasted_iota(
        jnp.int32, (tokens, tokens), 1
    )
    position = jnp.dot(
        member.astype(F32).astype(BF16),
        earlier.astype(F32).astype(BF16),
        preferred_element_type=F32,
    )
    return member & (position.astype(jnp.int32) == slot), named


def pick(group, ids, tokens, local_count):
    def kernel(group_ref, ids_ref, tokens_ref, out_ref):
        hit, _ = slot_hits(ids_ref[...], group_ref[0], local_count)
        rows = jnp.dot(
            hit.astype(F32).astype(BF16), tokens_ref[...], preferred_element_type=F32
        ).astype(BF16)
        for e in range(local_count):
            out_ref[e] = rows[e * CAP : (e + 1) * CAP]

    shape = jax.ShapeDtypeStruct((local_count, CAP, tokens.shape[1]), BF16)
    return call(kernel, "pick", shape, [group, ids, tokens], [SMEM, VMEM, VMEM], [])


def gate_up(place, rows, weights, start, width, after):
    local_count, _, depth = rows[0].shape
    count = sum(part.shape[1] for part in rows)
    pieces = 3
    block = depth // pieces

    def kernel(place_ref, *refs):
        row_refs, weight_refs = refs[: len(rows)], refs[len(rows) : len(rows) + 2]
        full_ref, short_ref, held, sems = refs[len(rows) + 2 :]
        copies = {}
        for at in range(2 * local_count):
            for k in range(pieces):
                copies[at, k] = pltpu.make_async_copy(
                    weight_refs[at % 2].at[at // 2, pl.ds(k * block, block), pl.ds(start, width)],
                    held.at[at, pl.ds(k * block, block), :],
                    sems.at[at * pieces + k],
                )
                copies[at, k].start()
        for e in range(local_count):
            x = jnp.concatenate([ref[e] for ref in row_refs], axis=0)
            for i in range(2):
                at = e * 2 + i
                for k in range(pieces):
                    copies[at, k].wait()
                full_ref[i, e] = jnp.dot(x, held[at], preferred_element_type=F32)

                @pl.when(place_ref[0] == 0)
                def _():
                    short_ref[i, e] = full_ref[i, e].astype(BF16)

    shape = (2, local_count, count, width)
    slots = 2 * local_count
    return call(
        kernel,
        "gate_up",
        [jax.ShapeDtypeStruct(shape, F32), jax.ShapeDtypeStruct(shape, BF16)],
        [place, *rows, *weights],
        [SMEM] + [VMEM] * len(rows) + [HBM, HBM],
        after,
        [pltpu.VMEM((slots, depth, width), BF16), pltpu.SemaphoreType.DMA((slots * pieces,))],
        limit=30,
    )


def add_to_send(place, at, full, got, after):
    def kernel(place_ref, full_ref, got_ref, out_ref):
        @pl.when(place_ref[0] == at)
        def _():
            for e in range(full_ref.shape[1]):
                for i in range(2):
                    out_ref[i, e] = (full_ref[i, e] + got_ref[i, e].astype(F32)).astype(BF16)

    shape = jax.ShapeDtypeStruct(full.shape, BF16)
    return call(kernel, "add_to_send", shape, [place, full, got], [SMEM, VMEM, VMEM], after)


def round_to_send(place, at, full, after):
    def kernel(place_ref, full_ref, out_ref):
        @pl.when(place_ref[0] == at)
        def _():
            out_ref[...] = full_ref[...].astype(BF16)

    shape = jax.ShapeDtypeStruct(full.shape, BF16)
    return call(kernel, "round_to_send", shape, [place, full], [SMEM, VMEM], after)


def hidden_values(place, at, full, got, after):
    widths = [part.shape[3] for part in full]
    flat = [value for values in got for value in values]
    arrivals = len(got[0])

    def kernel(place_ref, *refs):
        out_ref, got_refs = refs[-1], refs[len(widths) : -1]

        @pl.when(place_ref[0] == at)
        def _():
            start = 0
            for c, width in enumerate(widths):
                for e in range(out_ref.shape[0]):
                    gate, up = refs[c][0, e], refs[c][1, e]
                    for ref in got_refs[c * arrivals : (c + 1) * arrivals]:
                        gate, up = gate + ref[0, e].astype(F32), up + ref[1, e].astype(F32)
                    value = gate / (1.0 + jnp.exp(-gate)) * up
                    out_ref[e, :, start : start + width] = value.astype(BF16)
                start += width

    shape = jax.ShapeDtypeStruct(full[0].shape[1:3] + (sum(widths),), BF16)
    specs = [SMEM] + [VMEM] * (len(full) + len(flat))
    return call(kernel, "hidden_values", shape, [place, *full, *flat], specs, after)


def pass_on(value, after):
    def kernel(value_ref, out_ref):
        del value_ref, out_ref

    shape = jax.ShapeDtypeStruct(value.shape, value.dtype)
    return call(kernel, "pass_on", shape, [value], [ANY], after, aliases={0: 0})


def down(place, held, down_weight, starts, widths, totals, row_counts, after):
    local_count, count, _ = held[0].shape
    features = down_weight.shape[2]
    places = len(held)

    def kernel(place_ref, *refs):
        held_refs, weight_ref = refs[:places], refs[places]
        total_refs = refs[places + 1 : places + 1 + len(totals)]
        out_refs, hidden = refs[places + 1 + len(totals) : -1], refs[-1]
        for i in range(places):

            @pl.when(place_ref[0] == i)
            def _():
                hidden[...] = held_refs[i][...]

        for e in range(local_count):
            product, column = None, 0
            for start, width in zip(starts, widths):
                value = jnp.dot(
                    hidden[e, :, column : column + width],
                    weight_ref[e, start : start + width, :],
                    preferred_element_type=F32,
                )
                product = value if product is None else product + value
                column += width
            first = 0
            for i, rows in enumerate(row_counts):
                value = product[first : first + rows]
                out_refs[i][e] = total_refs[i][e] + value if totals else value
                first += rows

    return call(
        kernel,
        "down",
        [jax.ShapeDtypeStruct((local_count, rows, features), F32) for rows in row_counts],
        [place, *held, down_weight, *totals],
        [SMEM] + [VMEM] * (places + 1 + len(totals)),
        after,
        [pltpu.VMEM(held[0].shape, BF16)],
        limit=6 + 2 * local_count * count * features * 4 // MIB,
    )


def combine(group, ids, weights, sums, groups):
    local_count, _, features = sums[0].shape
    tokens = ids.shape[1]
    block = tokens // groups

    def kernel(group_ref, ids_ref, weights_ref, *refs):
        sum_refs, own_ref, sent = refs[: len(sums)], refs[len(sums)], refs[len(sums) + 1 :]
        hit, named = slot_hits(ids_ref[...], group_ref[0], local_count)
        scale = sum(
            jnp.where(named[k], weights_ref[k : k + 1, :], 0.0) for k in range(len(named))
        )
        scale = jnp.where(hit, scale, 0.0)
        scale_high = scale.astype(BF16)
        scale_low = (scale - scale_high.astype(F32)).astype(BF16)
        rows = jnp.concatenate(
            [functools.reduce(jnp.add, [ref[e] for ref in sum_refs]) for e in range(local_count)],
            axis=0,
        )
        rows_high = rows.astype(BF16)
        rows_low = (rows - rows_high.astype(F32)).astype(BF16)

        def product(a, b):
            return lax.dot_general(
                a, b, (((0,), (0,)), ((), ())), preferred_element_type=F32
            )

        mixed = (
            product(scale_high, rows_high)
            + product(scale_high, rows_low)
            + product(scale_low, rows_high)
        )
        for place in range(groups):
            piece = mixed[place * block : (place + 1) * block]
            step = group_ref[0] ^ place

            @pl.when(step == 0)
            def _():
                own_ref[...] = piece

            for other in range(1, groups):

                @pl.when(step == other)
                def _():
                    sent[other - 1][...] = piece.astype(BF16)

    return call(
        kernel,
        "combine",
        [jax.ShapeDtypeStruct((block, features), F32)]
        + [jax.ShapeDtypeStruct((block, features), BF16)] * (groups - 1),
        [group, ids, weights, *sums],
        [SMEM] + [VMEM] * (2 + len(sums)),
        [],
    )


def place_blocks(group, pieces):
    block, features = pieces[0].shape

    def kernel(group_ref, *refs):
        out_ref = refs[-1]
        for step, piece_ref in enumerate(refs[:-1]):
            start = pl.multiple_of((group_ref[0] ^ step) * block, block)
            out_ref[pl.ds(start, block), :] = piece_ref[...]

    shape = jax.ShapeDtypeStruct((block * len(pieces), features), BF16)
    return call(
        kernel, "place_blocks", shape, [group, *pieces], [SMEM] + [VMEM] * len(pieces), []
    )


def local(mesh_shape, tokens, expert_ids, route_weights, gate_weight, up_weight, down_weight):
    shards, groups, line = mesh_shape["dp"], mesh_shape["expert"], mesh_shape["blk"]
    local_count, _, hidden_count = gate_weight.shape
    group = lax.axis_index("expert").astype(jnp.int32).reshape(1)
    line_at = lax.axis_index("blk")
    odd = lax.axis_index("dp") % 2
    place = jnp.where(odd == 1, line - 1 - line_at, line_at).astype(jnp.int32).reshape(1)
    ids, choice_weights = expert_ids.T, route_weights.T
    swap = [(0, 1), (1, 0)]

    def hop(value, source, target):
        pairs = []
        for shard in range(shards):
            ends = (line - 1 - source, line - 1 - target) if shard % 2 else (source, target)
            pairs.append((shard * line + ends[0], shard * line + ends[1]))
        return lax.ppermute(value, ("dp", "blk"), pairs)

    rows = pick(group, ids, tokens, local_count)
    if shards == 2:
        rows = [rows, lax.ppermute(rows, "dp", swap)]
    else:
        rows = [lax.all_gather(rows, "dp", axis=1, tiled=True)]
    row_counts = [part.shape[1] for part in rows]

    widths = chunk_widths(hidden_count)
    starts = [sum(widths[:c]) for c in range(len(widths))]
    full, short, values, got, totals, after = {}, {}, {}, {}, [], []
    for name, c in ORDER:
        if c >= len(widths):
            continue
        kind = CHUNKS[c][1]
        owner, summed_by = OWNER[kind]
        chunks, way = GROUPS.get(c, ((), ""))
        chunks = [q for q in chunks if q < len(widths)]
        if name == "g":
            full[c], short[c] = gate_up(
                place, rows, (gate_weight, up_weight), starts[c], widths[c], after
            )
            after = [full[c]]
        elif name == "h":
            arrived = [[got[m, q] for m in summed_by] for q in chunks]
            values[c] = hidden_values(place, owner, [full[q] for q in chunks], arrived, after)
            after = [values[c]]
        elif name == "d":
            totals = down(
                place,
                [values[c] if m is None else got[m, c] for m in HELD[kind]],
                down_weight,
                [starts[q] for q in chunks],
                [widths[q] for q in chunks],
                totals,
                row_counts,
                after,
            )
            after = [totals[0]]
        else:
            route = SUMS[kind] if name[0] == "m" else BACK[kind, way]
            source, target, needed = route[name]
            if name == "m0":
                sent = short[c]
            elif name == "mb":
                sent = round_to_send(place, source, full[c], after)
                after = [sent]
            elif name[0] == "m":
                sent = add_to_send(place, source, full[c], got[needed, c], after)
                after = [sent]
            elif needed is None:
                sent = values[c]
            else:
                sent = got[needed, c] = pass_on(got[needed, c], after)
                after = [sent]
            got[name, c] = hop(sent, source, target)

    if shards == 2:
        sums = [totals[0], lax.ppermute(totals[1], "dp", swap)]
    else:
        sums = [lax.psum_scatter(totals[0], "dp", scatter_dimension=1, tiled=True)]
    own, *sent = combine(group, ids, choice_weights, sums, groups)
    for step in range(groups - 1, 0, -1):
        exchange = [(i, i ^ step) for i in range(groups)]
        own = own + lax.ppermute(sent[step - 1], "expert", exchange).astype(F32)
    block = own.astype(BF16)
    pieces = [block]
    for step in range(1, groups):
        pieces.append(lax.ppermute(block, "expert", [(i, i ^ step) for i in range(groups)]))
    return place_blocks(group, pieces)


def solution(mesh):
    placed = (
        P("dp", "blk"),
        P("dp", None),
        P("dp", None),
        P("expert", "blk", "dp"),
        P("expert", "blk", "dp"),
        P("expert", "dp", "blk"),
    )
    return jax.shard_map(
        functools.partial(local, dict(mesh.shape)),
        mesh=mesh,
        in_specs=placed,
        out_specs=P("dp", "blk"),
        check_vma=False,
    )
```

```python
import functools

import jax
import jax.numpy as jnp
from jax import lax
from jax.experimental import pallas as pl
from jax.experimental.pallas import tpu as pltpu
from jax.sharding import PartitionSpec as P

CAP = 48
F32, BF16 = jnp.float32, jnp.bfloat16
MIB = 1024 * 1024

CHUNKS = ((3, "end"), (3, "end"), (3, "end"), (3, "inner"), (2, "inner"), (2, "inner"))

ROUTES = {
    "end": {
        "m0": (0, 1, None), "m1": (1, 2, "m0"), "m2": (2, 3, "m1"),
        "a0": (3, 2, None), "a1": (2, 1, "a0"), "a2": (1, 0, "a1"),
    },
    "inner": {
        "m0": (0, 1, None), "mb": (3, 2, None), "m1": (1, 2, "m0"),
        "a0": (2, 1, None), "a1": (2, 3, None), "a2": (2, 0, None),
    },
}
OWNER = {"end": (3, ("m2",)), "inner": (2, ("m1", "mb"))}
HELD = {"end": ("a2", "a1", "a0", None), "inner": ("a2", "a0", None, "a1")}

ORDER = (
    ("g", 0), ("m0", 0), ("g", 2), ("m0", 2), ("g", 1), ("m0", 1), ("m1", 0), ("g", 3),
    ("m0", 3), ("m1", 2), ("g", 4), ("m0", 4), ("m1", 1), ("m2", 0), ("mb", 3), ("m1", 3),
    ("m2", 2), ("mb", 4), ("g", 5), ("m0", 5), ("m2", 1), ("h", 0), ("m1", 4), ("h", 3),
    ("a0", 0), ("a0", 3), ("h", 2), ("a0", 2), ("m1", 5), ("mb", 5), ("a1", 0), ("h", 4),
    ("a1", 3), ("a2", 3), ("a2", 4), ("a1", 2), ("h", 1), ("a0", 1), ("h", 5), ("a1", 5),
    ("a1", 4), ("a2", 0), ("a1", 1), ("a2", 2), ("a2", 5), ("a0", 5), ("a0", 4), ("a2", 1),
    ("d", 3), ("d", 0), ("d", 5), ("d", 2), ("d", 4), ("d", 1),
)

SMEM = pl.BlockSpec(memory_space=pltpu.SMEM)
VMEM = pl.BlockSpec(memory_space=pltpu.VMEM)
ANY = pl.BlockSpec(memory_space=pl.ANY)
HBM = pl.BlockSpec(memory_space=pltpu.HBM)


def call(kernel, name, outs, operands, specs, after, scratch=(), aliases=None, limit=6):
    count = len(operands)

    def body(*refs):
        kernel(*refs[:count], *refs[count + len(after) :])

    return pl.pallas_call(
        body,
        out_shape=outs,
        in_specs=list(specs) + [ANY] * len(after),
        out_specs=jax.tree.map(lambda _: VMEM, outs) if aliases is None else ANY,
        scratch_shapes=list(scratch),
        input_output_aliases=aliases or {},
        compiler_params=pltpu.CompilerParams(vmem_limit_bytes=limit * MIB),
        name=name,
    )(*operands, *after)


def chunk_widths(count):
    unit = 256 if count % 4096 == 0 else 128
    widths, start = [], 0
    for share, _ in CHUNKS:
        widths.append(max(unit, share * count // 16 // unit * unit))
    kept = []
    for width in widths:
        width = min(width, count - start)
        if width:
            kept.append(width)
        start += width
    kept[-1] += count - start
    return kept


def slot_hits(ids, group, local_count):
    tokens, lanes = ids.shape[1], local_count * CAP
    slot = lax.broadcasted_iota(jnp.int32, (lanes, tokens), 0)
    expert = jnp.full((lanes, tokens), group * local_count, jnp.int32)
    for step in range(1, local_count):
        passed = (slot >= CAP).astype(jnp.int32) if step == 1 else passed_next
        expert = expert + passed
        slot = slot - CAP * passed
        passed_next = (slot >= CAP).astype(jnp.int32)
    named = [ids[k : k + 1, :] == expert for k in range(ids.shape[0])]
    member = functools.reduce(jnp.logical_or, named)
    earlier = lax.broadcasted_iota(jnp.int32, (tokens, tokens), 0) < lax.broadcasted_iota(
        jnp.int32, (tokens, tokens), 1
    )
    position = jnp.dot(
        member.astype(F32).astype(BF16),
        earlier.astype(F32).astype(BF16),
        preferred_element_type=F32,
    )
    return member & (position.astype(jnp.int32) == slot), named


def pick(group, ids, tokens, local_count):
    def kernel(group_ref, ids_ref, tokens_ref, out_ref):
        hit, _ = slot_hits(ids_ref[...], group_ref[0], local_count)
        rows = jnp.dot(
            hit.astype(F32).astype(BF16), tokens_ref[...], preferred_element_type=F32
        ).astype(BF16)
        for e in range(local_count):
            out_ref[e] = rows[e * CAP : (e + 1) * CAP]

    shape = jax.ShapeDtypeStruct((local_count, CAP, tokens.shape[1]), BF16)
    return call(kernel, "pick", shape, [group, ids, tokens], [SMEM, VMEM, VMEM], [])


def gate_up(place, rows, weights, start, width, after):
    local_count, _, depth = rows[0].shape
    count = sum(part.shape[1] for part in rows)
    pieces = 3
    block = depth // pieces

    def kernel(place_ref, *refs):
        row_refs, weight_refs = refs[: len(rows)], refs[len(rows) : len(rows) + 2]
        full_ref, short_ref, held, sems = refs[len(rows) + 2 :]
        copies = {}
        for at in range(2 * local_count):
            for k in range(pieces):
                copies[at, k] = pltpu.make_async_copy(
                    weight_refs[at % 2].at[at // 2, pl.ds(k * block, block), pl.ds(start, width)],
                    held.at[at, pl.ds(k * block, block), :],
                    sems.at[at * pieces + k],
                )
                copies[at, k].start()
        for e in range(local_count):
            x = jnp.concatenate([ref[e] for ref in row_refs], axis=0)
            for i in range(2):
                at = e * 2 + i
                for k in range(pieces):
                    copies[at, k].wait()
                full_ref[i, e] = jnp.dot(x, held[at], preferred_element_type=F32)

                @pl.when(place_ref[0] == 0)
                def _():
                    short_ref[i, e] = full_ref[i, e].astype(BF16)

    shape = (2, local_count, count, width)
    slots = 2 * local_count
    return call(
        kernel,
        "gate_up",
        [jax.ShapeDtypeStruct(shape, F32), jax.ShapeDtypeStruct(shape, BF16)],
        [place, *rows, *weights],
        [SMEM] + [VMEM] * len(rows) + [HBM, HBM],
        after,
        [pltpu.VMEM((slots, depth, width), BF16), pltpu.SemaphoreType.DMA((slots * pieces,))],
        limit=30,
    )


def add_to_send(place, at, full, got, after):
    def kernel(place_ref, full_ref, got_ref, out_ref):
        @pl.when(place_ref[0] == at)
        def _():
            for e in range(full_ref.shape[1]):
                for i in range(2):
                    out_ref[i, e] = (full_ref[i, e] + got_ref[i, e].astype(F32)).astype(BF16)

    shape = jax.ShapeDtypeStruct(full.shape, BF16)
    return call(kernel, "add_to_send", shape, [place, full, got], [SMEM, VMEM, VMEM], after)


def round_to_send(place, at, full, after):
    def kernel(place_ref, full_ref, out_ref):
        @pl.when(place_ref[0] == at)
        def _():
            out_ref[...] = full_ref[...].astype(BF16)

    shape = jax.ShapeDtypeStruct(full.shape, BF16)
    return call(kernel, "round_to_send", shape, [place, full], [SMEM, VMEM], after)


def hidden_values(place, at, full, got, after):
    def kernel(place_ref, full_ref, *refs):
        got_refs, out_ref = refs[:-1], refs[-1]

        @pl.when(place_ref[0] == at)
        def _():
            for e in range(full_ref.shape[1]):
                gate, up = full_ref[0, e], full_ref[1, e]
                for ref in got_refs:
                    gate, up = gate + ref[0, e].astype(F32), up + ref[1, e].astype(F32)
                out_ref[e] = (gate / (1.0 + jnp.exp(-gate)) * up).astype(BF16)

    shape = jax.ShapeDtypeStruct(full.shape[1:], BF16)
    return call(
        kernel, "hidden_values", shape, [place, full, *got], [SMEM] + [VMEM] * (1 + len(got)), after
    )


def pass_on(value, after):
    def kernel(value_ref, out_ref):
        del value_ref, out_ref

    shape = jax.ShapeDtypeStruct(value.shape, value.dtype)
    return call(kernel, "pass_on", shape, [value], [ANY], after, aliases={0: 0})


def down(place, held, down_weight, start, totals, row_counts, after):
    local_count, count, width = held[0].shape
    features = down_weight.shape[2]
    block = 256 if width % 256 == 0 else 128
    pieces = width // block
    places = len(held)

    def kernel(place_ref, *refs):
        held_refs, weight_ref = refs[:places], refs[places]
        total_refs = refs[places + 1 : places + 1 + len(totals)]
        out_refs = refs[places + 1 + len(totals) :][: len(row_counts)]
        hidden = refs[-1]
        for i in range(places):

            @pl.when(place_ref[0] == i)
            def _():
                hidden[...] = held_refs[i][...]

        for e in range(local_count):
            product = None
            for k in range(pieces):
                part = jnp.dot(
                    hidden[e, :, k * block : (k + 1) * block],
                    weight_ref[e, start + k * block : start + (k + 1) * block, :],
                    preferred_element_type=F32,
                )
                product = part if product is None else product + part
            first = 0
            for i, rows in enumerate(row_counts):
                value = product[first : first + rows]
                out_refs[i][e] = total_refs[i][e] + value if totals else value
                first += rows

    shapes = [jax.ShapeDtypeStruct((local_count, rows, features), F32) for rows in row_counts]
    operands = [place, *held, down_weight, *totals]
    return call(
        kernel,
        "down",
        shapes,
        operands,
        [SMEM] + [VMEM] * (places + 1 + len(totals)),
        after,
        [
            pltpu.VMEM(held[0].shape, BF16),
        ],
        limit=6 + 2 * local_count * count * features * 4 // MIB,
    )


def combine(group, ids, weights, sums, groups):
    local_count, _, features = sums[0].shape
    tokens = ids.shape[1]
    block = tokens // groups

    def kernel(group_ref, ids_ref, weights_ref, *refs):
        sum_refs, own_ref, sent = refs[: len(sums)], refs[len(sums)], refs[len(sums) + 1 :]
        hit, named = slot_hits(ids_ref[...], group_ref[0], local_count)
        scale = sum(
            jnp.where(named[k], weights_ref[k : k + 1, :], 0.0) for k in range(len(named))
        )
        scale = jnp.where(hit, scale, 0.0)
        scale_high = scale.astype(BF16)
        scale_low = (scale - scale_high.astype(F32)).astype(BF16)
        rows = jnp.concatenate(
            [functools.reduce(jnp.add, [ref[e] for ref in sum_refs]) for e in range(local_count)],
            axis=0,
        )
        rows_high = rows.astype(BF16)
        rows_low = (rows - rows_high.astype(F32)).astype(BF16)

        def product(a, b):
            return lax.dot_general(
                a, b, (((0,), (0,)), ((), ())), preferred_element_type=F32
            )

        mixed = (
            product(scale_high, rows_high)
            + product(scale_high, rows_low)
            + product(scale_low, rows_high)
        )
        for place in range(groups):
            piece = mixed[place * block : (place + 1) * block]
            step = group_ref[0] ^ place

            @pl.when(step == 0)
            def _():
                own_ref[...] = piece

            for other in range(1, groups):

                @pl.when(step == other)
                def _():
                    sent[other - 1][...] = piece.astype(BF16)

    return call(
        kernel,
        "combine",
        [jax.ShapeDtypeStruct((block, features), F32)]
        + [jax.ShapeDtypeStruct((block, features), BF16)] * (groups - 1),
        [group, ids, weights, *sums],
        [SMEM] + [VMEM] * (2 + len(sums)),
        [],
    )


def place_blocks(group, pieces):
    block, features = pieces[0].shape

    def kernel(group_ref, *refs):
        out_ref = refs[-1]
        for step, piece_ref in enumerate(refs[:-1]):
            start = pl.multiple_of((group_ref[0] ^ step) * block, block)
            out_ref[pl.ds(start, block), :] = piece_ref[...]

    shape = jax.ShapeDtypeStruct((block * len(pieces), features), BF16)
    return call(
        kernel, "place_blocks", shape, [group, *pieces], [SMEM] + [VMEM] * len(pieces), []
    )


def local(mesh_shape, tokens, expert_ids, route_weights, gate_weight, up_weight, down_weight):
    shards, groups, line = mesh_shape["dp"], mesh_shape["expert"], mesh_shape["blk"]
    local_count, _, hidden_count = gate_weight.shape
    group = lax.axis_index("expert").astype(jnp.int32).reshape(1)
    line_at = lax.axis_index("blk")
    odd = lax.axis_index("dp") % 2
    place = jnp.where(odd == 1, line - 1 - line_at, line_at).astype(jnp.int32).reshape(1)
    ids, choice_weights = expert_ids.T, route_weights.T
    swap = [(0, 1), (1, 0)]

    def hop(value, source, target):
        pairs = []
        for shard in range(shards):
            ends = (line - 1 - source, line - 1 - target) if shard % 2 else (source, target)
            pairs.append((shard * line + ends[0], shard * line + ends[1]))
        return lax.ppermute(value, ("dp", "blk"), pairs)

    rows = pick(group, ids, tokens, local_count)
    if shards == 2:
        rows = [rows, lax.ppermute(rows, "dp", swap)]
    else:
        rows = [lax.all_gather(rows, "dp", axis=1, tiled=True)]
    row_counts = [part.shape[1] for part in rows]

    widths = chunk_widths(hidden_count)
    starts = [sum(widths[:c]) for c in range(len(widths))]
    full, short, values, got, totals, after = {}, {}, {}, {}, [], []
    for name, c in ORDER:
        if c >= len(widths):
            continue
        kind = CHUNKS[c][1]
        route = ROUTES[kind]
        owner, summed_by = OWNER[kind]
        if name == "g":
            full[c], short[c] = gate_up(
                place, rows, (gate_weight, up_weight), starts[c], widths[c], after
            )
            after = [full[c]]
        elif name == "h":
            values[c] = hidden_values(place, owner, full[c], [got[c, m] for m in summed_by], after)
            after = [values[c]]
        elif name == "d":
            held = [values[c] if m is None else got[c, m] for m in HELD[kind]]
            totals = down(place, held, down_weight, starts[c], totals, row_counts, after)
            after = [totals[0]]
        else:
            source, target, needed = route[name]
            if name == "m0":
                sent = short[c]
            elif name == "mb":
                sent = round_to_send(place, source, full[c], after)
                after = [sent]
            elif name[0] == "m":
                sent = add_to_send(place, source, full[c], got[c, needed], after)
                after = [sent]
            elif needed is None:
                sent = values[c]
            else:
                sent = got[c, needed] = pass_on(got[c, needed], after)
                after = [sent]
            got[c, name] = hop(sent, source, target)

    if shards == 2:
        sums = [totals[0], lax.ppermute(totals[1], "dp", swap)]
    else:
        sums = [lax.psum_scatter(totals[0], "dp", scatter_dimension=1, tiled=True)]
    own, *sent = combine(group, ids, choice_weights, sums, groups)
    for step in range(groups - 1, 0, -1):
        exchange = [(i, i ^ step) for i in range(groups)]
        own = own + lax.ppermute(sent[step - 1], "expert", exchange).astype(F32)
    block = own.astype(BF16)
    pieces = [block]
    for step in range(1, groups):
        pieces.append(lax.ppermute(block, "expert", [(i, i ^ step) for i in range(groups)]))
    return place_blocks(group, pieces)


def solution(mesh):
    placed = (
        P("dp", "blk"),
        P("dp", None),
        P("dp", None),
        P("expert", "blk", "dp"),
        P("expert", "blk", "dp"),
        P("expert", "dp", "blk"),
    )
    return jax.shard_map(
        functools.partial(local, dict(mesh.shape)),
        mesh=mesh,
        in_specs=placed,
        out_specs=P("dp", "blk"),
        check_vma=False,
    )
```

```python
import functools

import jax
import jax.numpy as jnp
from jax import lax
from jax.experimental import pallas as pl
from jax.experimental.pallas import tpu as pltpu
from jax.sharding import PartitionSpec as P

CAP = 48
F32, BF16 = jnp.float32, jnp.bfloat16
MIB = 1024 * 1024

CHUNKS = ((4, "end"), (4, "end"), (4, "inner"), (4, "inner"))
GROUPS = {0: ((0,), "relay"), 1: ((1,), "relay"), 2: ((2,), "direct"), 3: ((3,), "direct")}

SUMS = {
    "end": {"m0": (0, 1, None), "m1": (1, 2, "m0"), "m2": (2, 3, "m1")},
    "inner": {"m0": (0, 1, None), "mb": (3, 2, None), "m1": (1, 2, "m0")},
}
BACK = {
    ("end", "relay"): {"a0": (3, 2, None), "a1": (2, 1, "a0"), "a2": (1, 0, "a1")},
    ("end", "direct"): {"a0": (3, 2, None), "a1": (3, 1, None), "a2": (3, 0, None)},
    ("inner", "relay"): {"a0": (2, 1, None), "a1": (2, 3, None), "a2": (1, 0, "a0")},
    ("inner", "direct"): {"a0": (2, 1, None), "a1": (2, 3, None), "a2": (2, 0, None)},
}
OWNER = {"end": (3, ("m2",)), "inner": (2, ("m1", "mb"))}
HELD = {"end": ("a2", "a1", "a0", None), "inner": ("a2", "a0", None, "a1")}

ORDER = (
    ("g", 0), ("m0", 0), ("g", 1), ("m0", 1), ("g", 3), ("m0", 3), ("m1", 0), ("g", 2),
    ("m0", 2), ("m1", 1), ("m2", 0), ("mb", 3), ("mb", 2), ("m1", 3), ("m2", 1), ("m1", 2),
    ("h", 0), ("h", 3), ("h", 1), ("a0", 1), ("h", 2), ("a0", 3), ("a1", 3), ("a2", 3),
    ("a1", 2), ("d", 3), ("a1", 1), ("a0", 2), ("a2", 2), ("d", 2), ("a0", 0), ("a1", 0),
    ("a2", 1), ("a2", 0), ("d", 1), ("d", 0),
)

SMEM = pl.BlockSpec(memory_space=pltpu.SMEM)
VMEM = pl.BlockSpec(memory_space=pltpu.VMEM)
ANY = pl.BlockSpec(memory_space=pl.ANY)
HBM = pl.BlockSpec(memory_space=pltpu.HBM)


def call(kernel, name, outs, operands, specs, after, scratch=(), aliases=None, limit=6):
    count = len(operands)

    def body(*refs):
        kernel(*refs[:count], *refs[count + len(after) :])

    return pl.pallas_call(
        body,
        out_shape=outs,
        in_specs=list(specs) + [ANY] * len(after),
        out_specs=jax.tree.map(lambda _: VMEM, outs) if aliases is None else ANY,
        scratch_shapes=list(scratch),
        input_output_aliases=aliases or {},
        compiler_params=pltpu.CompilerParams(vmem_limit_bytes=limit * MIB),
        name=name,
    )(*operands, *after)


def chunk_widths(count):
    unit = 256 if count % 4096 == 0 else 128
    widths, start = [], 0
    for share, _ in CHUNKS:
        widths.append(max(unit, share * count // 16 // unit * unit))
    kept = []
    for width in widths:
        width = min(width, count - start)
        if width:
            kept.append(width)
        start += width
    kept[-1] += count - start
    return kept


def slot_hits(ids, group, local_count):
    tokens, lanes = ids.shape[1], local_count * CAP
    slot = lax.broadcasted_iota(jnp.int32, (lanes, tokens), 0)
    expert = jnp.full((lanes, tokens), group * local_count, jnp.int32)
    for step in range(1, local_count):
        passed = (slot >= CAP).astype(jnp.int32) if step == 1 else passed_next
        expert = expert + passed
        slot = slot - CAP * passed
        passed_next = (slot >= CAP).astype(jnp.int32)
    named = [ids[k : k + 1, :] == expert for k in range(ids.shape[0])]
    member = functools.reduce(jnp.logical_or, named)
    earlier = lax.broadcasted_iota(jnp.int32, (tokens, tokens), 0) < lax.broadcasted_iota(
        jnp.int32, (tokens, tokens), 1
    )
    position = jnp.dot(
        member.astype(F32).astype(BF16),
        earlier.astype(F32).astype(BF16),
        preferred_element_type=F32,
    )
    return member & (position.astype(jnp.int32) == slot), named


def pick(group, ids, tokens, local_count):
    def kernel(group_ref, ids_ref, tokens_ref, out_ref):
        hit, _ = slot_hits(ids_ref[...], group_ref[0], local_count)
        rows = jnp.dot(
            hit.astype(F32).astype(BF16), tokens_ref[...], preferred_element_type=F32
        ).astype(BF16)
        for e in range(local_count):
            out_ref[e] = rows[e * CAP : (e + 1) * CAP]

    shape = jax.ShapeDtypeStruct((local_count, CAP, tokens.shape[1]), BF16)
    return call(kernel, "pick", shape, [group, ids, tokens], [SMEM, VMEM, VMEM], [])


def gate_up(place, rows, weights, start, width, after):
    local_count, _, depth = rows[0].shape
    count = sum(part.shape[1] for part in rows)
    pieces = 3
    block = depth // pieces

    def kernel(place_ref, *refs):
        row_refs, weight_refs = refs[: len(rows)], refs[len(rows) : len(rows) + 2]
        full_ref, short_ref, held, sems = refs[len(rows) + 2 :]
        copies = {}
        for at in range(2 * local_count):
            for k in range(pieces):
                copies[at, k] = pltpu.make_async_copy(
                    weight_refs[at % 2].at[at // 2, pl.ds(k * block, block), pl.ds(start, width)],
                    held.at[at, pl.ds(k * block, block), :],
                    sems.at[at * pieces + k],
                )
                copies[at, k].start()
        for e in range(local_count):
            x = jnp.concatenate([ref[e] for ref in row_refs], axis=0)
            for i in range(2):
                at = e * 2 + i
                for k in range(pieces):
                    copies[at, k].wait()
                full_ref[i, e] = jnp.dot(x, held[at], preferred_element_type=F32)

                @pl.when(place_ref[0] == 0)
                def _():
                    short_ref[i, e] = full_ref[i, e].astype(BF16)

    shape = (2, local_count, count, width)
    slots = 2 * local_count
    return call(
        kernel,
        "gate_up",
        [jax.ShapeDtypeStruct(shape, F32), jax.ShapeDtypeStruct(shape, BF16)],
        [place, *rows, *weights],
        [SMEM] + [VMEM] * len(rows) + [HBM, HBM],
        after,
        [pltpu.VMEM((slots, depth, width), BF16), pltpu.SemaphoreType.DMA((slots * pieces,))],
        limit=30,
    )


def add_to_send(place, at, full, got, after):
    def kernel(place_ref, full_ref, got_ref, out_ref):
        @pl.when(place_ref[0] == at)
        def _():
            for e in range(full_ref.shape[1]):
                for i in range(2):
                    out_ref[i, e] = (full_ref[i, e] + got_ref[i, e].astype(F32)).astype(BF16)

    shape = jax.ShapeDtypeStruct(full.shape, BF16)
    return call(kernel, "add_to_send", shape, [place, full, got], [SMEM, VMEM, VMEM], after)


def round_to_send(place, at, full, after):
    def kernel(place_ref, full_ref, out_ref):
        @pl.when(place_ref[0] == at)
        def _():
            out_ref[...] = full_ref[...].astype(BF16)

    shape = jax.ShapeDtypeStruct(full.shape, BF16)
    return call(kernel, "round_to_send", shape, [place, full], [SMEM, VMEM], after)


def hidden_values(place, at, full, got, after):
    widths = [part.shape[3] for part in full]
    flat = [value for values in got for value in values]
    arrivals = len(got[0])

    def kernel(place_ref, *refs):
        out_ref, got_refs = refs[-1], refs[len(widths) : -1]

        @pl.when(place_ref[0] == at)
        def _():
            start = 0
            for c, width in enumerate(widths):
                for e in range(out_ref.shape[0]):
                    gate, up = refs[c][0, e], refs[c][1, e]
                    for ref in got_refs[c * arrivals : (c + 1) * arrivals]:
                        gate, up = gate + ref[0, e].astype(F32), up + ref[1, e].astype(F32)
                    value = gate / (1.0 + jnp.exp(-gate)) * up
                    out_ref[e, :, start : start + width] = value.astype(BF16)
                start += width

    shape = jax.ShapeDtypeStruct(full[0].shape[1:3] + (sum(widths),), BF16)
    specs = [SMEM] + [VMEM] * (len(full) + len(flat))
    return call(kernel, "hidden_values", shape, [place, *full, *flat], specs, after)


def pass_on(value, after):
    def kernel(value_ref, out_ref):
        del value_ref, out_ref

    shape = jax.ShapeDtypeStruct(value.shape, value.dtype)
    return call(kernel, "pass_on", shape, [value], [ANY], after, aliases={0: 0})


def down(place, held, down_weight, starts, widths, totals, row_counts, after):
    local_count, count, _ = held[0].shape
    features = down_weight.shape[2]
    places = len(held)

    def kernel(place_ref, *refs):
        held_refs, weight_ref = refs[:places], refs[places]
        total_refs = refs[places + 1 : places + 1 + len(totals)]
        out_refs, hidden = refs[places + 1 + len(totals) : -1], refs[-1]
        for i in range(places):

            @pl.when(place_ref[0] == i)
            def _():
                hidden[...] = held_refs[i][...]

        for e in range(local_count):
            product, column = None, 0
            for start, width in zip(starts, widths):
                value = jnp.dot(
                    hidden[e, :, column : column + width],
                    weight_ref[e, start : start + width, :],
                    preferred_element_type=F32,
                )
                product = value if product is None else product + value
                column += width
            first = 0
            for i, rows in enumerate(row_counts):
                value = product[first : first + rows]
                out_refs[i][e] = total_refs[i][e] + value if totals else value
                first += rows

    return call(
        kernel,
        "down",
        [jax.ShapeDtypeStruct((local_count, rows, features), F32) for rows in row_counts],
        [place, *held, down_weight, *totals],
        [SMEM] + [VMEM] * (places + 1 + len(totals)),
        after,
        [pltpu.VMEM(held[0].shape, BF16)],
        limit=6 + 2 * local_count * count * features * 4 // MIB,
    )


def combine(group, ids, weights, sums, groups):
    local_count, _, features = sums[0].shape
    tokens = ids.shape[1]
    block = tokens // groups

    def kernel(group_ref, ids_ref, weights_ref, *refs):
        sum_refs, own_ref, sent = refs[: len(sums)], refs[len(sums)], refs[len(sums) + 1 :]
        hit, named = slot_hits(ids_ref[...], group_ref[0], local_count)
        scale = sum(
            jnp.where(named[k], weights_ref[k : k + 1, :], 0.0) for k in range(len(named))
        )
        scale = jnp.where(hit, scale, 0.0)
        scale_high = scale.astype(BF16)
        scale_low = (scale - scale_high.astype(F32)).astype(BF16)
        rows = jnp.concatenate(
            [functools.reduce(jnp.add, [ref[e] for ref in sum_refs]) for e in range(local_count)],
            axis=0,
        )
        rows_high = rows.astype(BF16)
        rows_low = (rows - rows_high.astype(F32)).astype(BF16)

        def product(a, b):
            return lax.dot_general(
                a, b, (((0,), (0,)), ((), ())), preferred_element_type=F32
            )

        mixed = (
            product(scale_high, rows_high)
            + product(scale_high, rows_low)
            + product(scale_low, rows_high)
        )
        for place in range(groups):
            piece = mixed[place * block : (place + 1) * block]
            step = group_ref[0] ^ place

            @pl.when(step == 0)
            def _():
                own_ref[...] = piece

            for other in range(1, groups):

                @pl.when(step == other)
                def _():
                    sent[other - 1][...] = piece.astype(BF16)

    return call(
        kernel,
        "combine",
        [jax.ShapeDtypeStruct((block, features), F32)]
        + [jax.ShapeDtypeStruct((block, features), BF16)] * (groups - 1),
        [group, ids, weights, *sums],
        [SMEM] + [VMEM] * (2 + len(sums)),
        [],
    )


def place_blocks(group, pieces):
    block, features = pieces[0].shape

    def kernel(group_ref, *refs):
        out_ref = refs[-1]
        for step, piece_ref in enumerate(refs[:-1]):
            start = pl.multiple_of((group_ref[0] ^ step) * block, block)
            out_ref[pl.ds(start, block), :] = piece_ref[...]

    shape = jax.ShapeDtypeStruct((block * len(pieces), features), BF16)
    return call(
        kernel, "place_blocks", shape, [group, *pieces], [SMEM] + [VMEM] * len(pieces), []
    )


def local(mesh_shape, tokens, expert_ids, route_weights, gate_weight, up_weight, down_weight):
    shards, groups, line = mesh_shape["dp"], mesh_shape["expert"], mesh_shape["blk"]
    local_count, _, hidden_count = gate_weight.shape
    group = lax.axis_index("expert").astype(jnp.int32).reshape(1)
    line_at = lax.axis_index("blk")
    odd = lax.axis_index("dp") % 2
    place = jnp.where(odd == 1, line - 1 - line_at, line_at).astype(jnp.int32).reshape(1)
    ids, choice_weights = expert_ids.T, route_weights.T
    swap = [(0, 1), (1, 0)]

    def hop(value, source, target):
        pairs = []
        for shard in range(shards):
            ends = (line - 1 - source, line - 1 - target) if shard % 2 else (source, target)
            pairs.append((shard * line + ends[0], shard * line + ends[1]))
        return lax.ppermute(value, ("dp", "blk"), pairs)

    rows = pick(group, ids, tokens, local_count)
    if shards == 2:
        rows = [rows, lax.ppermute(rows, "dp", swap)]
    else:
        rows = [lax.all_gather(rows, "dp", axis=1, tiled=True)]
    row_counts = [part.shape[1] for part in rows]

    widths = chunk_widths(hidden_count)
    starts = [sum(widths[:c]) for c in range(len(widths))]
    full, short, values, got, totals, after = {}, {}, {}, {}, [], []
    for name, c in ORDER:
        if c >= len(widths):
            continue
        kind = CHUNKS[c][1]
        owner, summed_by = OWNER[kind]
        chunks, way = GROUPS.get(c, ((), ""))
        chunks = [q for q in chunks if q < len(widths)]
        if name == "g":
            full[c], short[c] = gate_up(
                place, rows, (gate_weight, up_weight), starts[c], widths[c], after
            )
            after = [full[c]]
        elif name == "h":
            arrived = [[got[m, q] for m in summed_by] for q in chunks]
            values[c] = hidden_values(place, owner, [full[q] for q in chunks], arrived, after)
            after = [values[c]]
        elif name == "d":
            totals = down(
                place,
                [values[c] if m is None else got[m, c] for m in HELD[kind]],
                down_weight,
                [starts[q] for q in chunks],
                [widths[q] for q in chunks],
                totals,
                row_counts,
                after,
            )
            after = [totals[0]]
        else:
            route = SUMS[kind] if name[0] == "m" else BACK[kind, way]
            source, target, needed = route[name]
            if name == "m0":
                sent = short[c]
            elif name == "mb":
                sent = round_to_send(place, source, full[c], after)
                after = [sent]
            elif name[0] == "m":
                sent = add_to_send(place, source, full[c], got[needed, c], after)
                after = [sent]
            elif needed is None:
                sent = values[c]
            else:
                sent = got[needed, c] = pass_on(got[needed, c], after)
                after = [sent]
            got[name, c] = hop(sent, source, target)

    if shards == 2:
        sums = [totals[0], lax.ppermute(totals[1], "dp", swap)]
    else:
        sums = [lax.psum_scatter(totals[0], "dp", scatter_dimension=1, tiled=True)]
    own, *sent = combine(group, ids, choice_weights, sums, groups)
    for step in range(groups - 1, 0, -1):
        exchange = [(i, i ^ step) for i in range(groups)]
        own = own + lax.ppermute(sent[step - 1], "expert", exchange).astype(F32)
    block = own.astype(BF16)
    pieces = [block]
    for step in range(1, groups):
        pieces.append(lax.ppermute(block, "expert", [(i, i ^ step) for i in range(groups)]))
    return place_blocks(group, pieces)


def solution(mesh):
    placed = (
        P("dp", "blk"),
        P("dp", None),
        P("dp", None),
        P("expert", "blk", "dp"),
        P("expert", "blk", "dp"),
        P("expert", "dp", "blk"),
    )
    return jax.shard_map(
        functools.partial(local, dict(mesh.shape)),
        mesh=mesh,
        in_specs=placed,
        out_specs=P("dp", "blk"),
        check_vma=False,
    )
```

```python
import functools

import jax
import jax.numpy as jnp
from jax import lax
from jax.experimental import pallas as pl
from jax.experimental.pallas import tpu as pltpu
from jax.sharding import PartitionSpec as P

CAP = 48
F32, BF16 = jnp.float32, jnp.bfloat16
MIB = 1024 * 1024

CHUNKS = ((4, "end"), (4, "end"), (4, "inner"), (4, "inner"))
GROUPS = {0: ((0,), "relay"), 1: ((1,), "relay"), 2: ((2,), "relay"), 3: ((3,), "relay")}

SUMS = {
    "end": {"m0": (0, 1, None), "m1": (1, 2, "m0"), "m2": (2, 3, "m1")},
    "inner": {"m0": (0, 1, None), "mb": (3, 2, None), "m1": (1, 2, "m0")},
}
BACK = {
    ("end", "relay"): {"a0": (3, 2, None), "a1": (2, 1, "a0"), "a2": (1, 0, "a1")},
    ("end", "direct"): {"a0": (3, 2, None), "a1": (3, 1, None), "a2": (3, 0, None)},
    ("inner", "relay"): {"a0": (2, 1, None), "a1": (2, 3, None), "a2": (1, 0, "a0")},
    ("inner", "direct"): {"a0": (2, 1, None), "a1": (2, 3, None), "a2": (2, 0, None)},
}
OWNER = {"end": (3, ("m2",)), "inner": (2, ("m1", "mb"))}
HELD = {"end": ("a2", "a1", "a0", None), "inner": ("a2", "a0", None, "a1")}

ORDER = (
    ("g", 1), ("m0", 1), ("g", 0), ("m0", 0), ("g", 3), ("m0", 3), ("m1", 1), ("g", 2),
    ("m0", 2), ("m1", 0), ("m2", 1), ("m1", 3), ("mb", 2), ("mb", 3), ("m2", 0), ("m1", 2),
    ("h", 1), ("h", 3), ("h", 0), ("h", 2), ("a0", 3), ("a0", 1), ("a2", 3), ("a0", 0),
    ("a0", 2), ("a1", 0), ("a1", 1), ("a1", 3), ("d", 3), ("a2", 2), ("a2", 0), ("a1", 2),
    ("a2", 1), ("d", 2), ("d", 0), ("d", 1),
)

SMEM = pl.BlockSpec(memory_space=pltpu.SMEM)
VMEM = pl.BlockSpec(memory_space=pltpu.VMEM)
ANY = pl.BlockSpec(memory_space=pl.ANY)
HBM = pl.BlockSpec(memory_space=pltpu.HBM)


def call(kernel, name, outs, operands, specs, after, scratch=(), aliases=None, limit=6):
    count = len(operands)

    def body(*refs):
        kernel(*refs[:count], *refs[count + len(after) :])

    return pl.pallas_call(
        body,
        out_shape=outs,
        in_specs=list(specs) + [ANY] * len(after),
        out_specs=jax.tree.map(lambda _: VMEM, outs) if aliases is None else ANY,
        scratch_shapes=list(scratch),
        input_output_aliases=aliases or {},
        compiler_params=pltpu.CompilerParams(vmem_limit_bytes=limit * MIB),
        name=name,
    )(*operands, *after)


def chunk_widths(count):
    unit = 256 if count % 4096 == 0 else 128
    widths, start = [], 0
    for share, _ in CHUNKS:
        widths.append(max(unit, share * count // 16 // unit * unit))
    kept = []
    for width in widths:
        width = min(width, count - start)
        if width:
            kept.append(width)
        start += width
    kept[-1] += count - start
    return kept


def slot_hits(ids, group, local_count):
    tokens, lanes = ids.shape[1], local_count * CAP
    slot = lax.broadcasted_iota(jnp.int32, (lanes, tokens), 0)
    expert = jnp.full((lanes, tokens), group * local_count, jnp.int32)
    for step in range(1, local_count):
        passed = (slot >= CAP).astype(jnp.int32) if step == 1 else passed_next
        expert = expert + passed
        slot = slot - CAP * passed
        passed_next = (slot >= CAP).astype(jnp.int32)
    named = [ids[k : k + 1, :] == expert for k in range(ids.shape[0])]
    member = functools.reduce(jnp.logical_or, named)
    earlier = lax.broadcasted_iota(jnp.int32, (tokens, tokens), 0) < lax.broadcasted_iota(
        jnp.int32, (tokens, tokens), 1
    )
    position = jnp.dot(
        member.astype(F32).astype(BF16),
        earlier.astype(F32).astype(BF16),
        preferred_element_type=F32,
    )
    return member & (position.astype(jnp.int32) == slot), named


def pick(group, ids, tokens, local_count):
    def kernel(group_ref, ids_ref, tokens_ref, out_ref):
        hit, _ = slot_hits(ids_ref[...], group_ref[0], local_count)
        rows = jnp.dot(
            hit.astype(F32).astype(BF16), tokens_ref[...], preferred_element_type=F32
        ).astype(BF16)
        for e in range(local_count):
            out_ref[e] = rows[e * CAP : (e + 1) * CAP]

    shape = jax.ShapeDtypeStruct((local_count, CAP, tokens.shape[1]), BF16)
    return call(kernel, "pick", shape, [group, ids, tokens], [SMEM, VMEM, VMEM], [])


def gate_up(place, rows, weights, start, width, after):
    local_count, _, depth = rows[0].shape
    count = sum(part.shape[1] for part in rows)
    pieces = 3
    block = depth // pieces

    def kernel(place_ref, *refs):
        row_refs, weight_refs = refs[: len(rows)], refs[len(rows) : len(rows) + 2]
        full_ref, short_ref, held, sems = refs[len(rows) + 2 :]
        copies = {}
        for at in range(2 * local_count):
            for k in range(pieces):
                copies[at, k] = pltpu.make_async_copy(
                    weight_refs[at % 2].at[at // 2, pl.ds(k * block, block), pl.ds(start, width)],
                    held.at[at, pl.ds(k * block, block), :],
                    sems.at[at * pieces + k],
                )
                copies[at, k].start()
        for e in range(local_count):
            x = jnp.concatenate([ref[e] for ref in row_refs], axis=0)
            for i in range(2):
                at = e * 2 + i
                for k in range(pieces):
                    copies[at, k].wait()
                full_ref[i, e] = jnp.dot(x, held[at], preferred_element_type=F32)

                @pl.when(place_ref[0] == 0)
                def _():
                    short_ref[i, e] = full_ref[i, e].astype(BF16)

    shape = (2, local_count, count, width)
    slots = 2 * local_count
    return call(
        kernel,
        "gate_up",
        [jax.ShapeDtypeStruct(shape, F32), jax.ShapeDtypeStruct(shape, BF16)],
        [place, *rows, *weights],
        [SMEM] + [VMEM] * len(rows) + [HBM, HBM],
        after,
        [pltpu.VMEM((slots, depth, width), BF16), pltpu.SemaphoreType.DMA((slots * pieces,))],
        limit=30,
    )


def add_to_send(place, at, full, got, after):
    def kernel(place_ref, full_ref, got_ref, out_ref):
        @pl.when(place_ref[0] == at)
        def _():
            for e in range(full_ref.shape[1]):
                for i in range(2):
                    out_ref[i, e] = (full_ref[i, e] + got_ref[i, e].astype(F32)).astype(BF16)

    shape = jax.ShapeDtypeStruct(full.shape, BF16)
    return call(kernel, "add_to_send", shape, [place, full, got], [SMEM, VMEM, VMEM], after)


def round_to_send(place, at, full, after):
    def kernel(place_ref, full_ref, out_ref):
        @pl.when(place_ref[0] == at)
        def _():
            out_ref[...] = full_ref[...].astype(BF16)

    shape = jax.ShapeDtypeStruct(full.shape, BF16)
    return call(kernel, "round_to_send", shape, [place, full], [SMEM, VMEM], after)


def hidden_values(place, at, full, got, after):
    widths = [part.shape[3] for part in full]
    flat = [value for values in got for value in values]
    arrivals = len(got[0])

    def kernel(place_ref, *refs):
        out_ref, got_refs = refs[-1], refs[len(widths) : -1]

        @pl.when(place_ref[0] == at)
        def _():
            start = 0
            for c, width in enumerate(widths):
                for e in range(out_ref.shape[0]):
                    gate, up = refs[c][0, e], refs[c][1, e]
                    for ref in got_refs[c * arrivals : (c + 1) * arrivals]:
                        gate, up = gate + ref[0, e].astype(F32), up + ref[1, e].astype(F32)
                    value = gate / (1.0 + jnp.exp(-gate)) * up
                    out_ref[e, :, start : start + width] = value.astype(BF16)
                start += width

    shape = jax.ShapeDtypeStruct(full[0].shape[1:3] + (sum(widths),), BF16)
    specs = [SMEM] + [VMEM] * (len(full) + len(flat))
    return call(kernel, "hidden_values", shape, [place, *full, *flat], specs, after)


def pass_on(value, after):
    def kernel(value_ref, out_ref):
        del value_ref, out_ref

    shape = jax.ShapeDtypeStruct(value.shape, value.dtype)
    return call(kernel, "pass_on", shape, [value], [ANY], after, aliases={0: 0})


def down(place, held, down_weight, starts, widths, totals, row_counts, after):
    local_count, count, _ = held[0].shape
    features = down_weight.shape[2]
    places = len(held)

    def kernel(place_ref, *refs):
        held_refs, weight_ref = refs[:places], refs[places]
        total_refs = refs[places + 1 : places + 1 + len(totals)]
        out_refs, hidden = refs[places + 1 + len(totals) : -1], refs[-1]
        for i in range(places):

            @pl.when(place_ref[0] == i)
            def _():
                hidden[...] = held_refs[i][...]

        for e in range(local_count):
            product, column = None, 0
            for start, width in zip(starts, widths):
                value = jnp.dot(
                    hidden[e, :, column : column + width],
                    weight_ref[e, start : start + width, :],
                    preferred_element_type=F32,
                )
                product = value if product is None else product + value
                column += width
            first = 0
            for i, rows in enumerate(row_counts):
                value = product[first : first + rows]
                out_refs[i][e] = total_refs[i][e] + value if totals else value
                first += rows

    return call(
        kernel,
        "down",
        [jax.ShapeDtypeStruct((local_count, rows, features), F32) for rows in row_counts],
        [place, *held, down_weight, *totals],
        [SMEM] + [VMEM] * (places + 1 + len(totals)),
        after,
        [pltpu.VMEM(held[0].shape, BF16)],
        limit=6 + 2 * local_count * count * features * 4 // MIB,
    )


def combine(group, ids, weights, sums, groups):
    local_count, _, features = sums[0].shape
    tokens = ids.shape[1]
    block = tokens // groups

    def kernel(group_ref, ids_ref, weights_ref, *refs):
        sum_refs, own_ref, sent = refs[: len(sums)], refs[len(sums)], refs[len(sums) + 1 :]
        hit, named = slot_hits(ids_ref[...], group_ref[0], local_count)
        scale = sum(
            jnp.where(named[k], weights_ref[k : k + 1, :], 0.0) for k in range(len(named))
        )
        scale = jnp.where(hit, scale, 0.0)
        scale_high = scale.astype(BF16)
        scale_low = (scale - scale_high.astype(F32)).astype(BF16)
        rows = jnp.concatenate(
            [functools.reduce(jnp.add, [ref[e] for ref in sum_refs]) for e in range(local_count)],
            axis=0,
        )
        rows_high = rows.astype(BF16)
        rows_low = (rows - rows_high.astype(F32)).astype(BF16)

        def product(a, b):
            return lax.dot_general(
                a, b, (((0,), (0,)), ((), ())), preferred_element_type=F32
            )

        mixed = (
            product(scale_high, rows_high)
            + product(scale_high, rows_low)
            + product(scale_low, rows_high)
        )
        for place in range(groups):
            piece = mixed[place * block : (place + 1) * block]
            step = group_ref[0] ^ place

            @pl.when(step == 0)
            def _():
                own_ref[...] = piece

            for other in range(1, groups):

                @pl.when(step == other)
                def _():
                    sent[other - 1][...] = piece.astype(BF16)

    return call(
        kernel,
        "combine",
        [jax.ShapeDtypeStruct((block, features), F32)]
        + [jax.ShapeDtypeStruct((block, features), BF16)] * (groups - 1),
        [group, ids, weights, *sums],
        [SMEM] + [VMEM] * (2 + len(sums)),
        [],
    )


def place_blocks(group, pieces):
    block, features = pieces[0].shape

    def kernel(group_ref, *refs):
        out_ref = refs[-1]
        for step, piece_ref in enumerate(refs[:-1]):
            start = pl.multiple_of((group_ref[0] ^ step) * block, block)
            out_ref[pl.ds(start, block), :] = piece_ref[...]

    shape = jax.ShapeDtypeStruct((block * len(pieces), features), BF16)
    return call(
        kernel, "place_blocks", shape, [group, *pieces], [SMEM] + [VMEM] * len(pieces), []
    )


def local(mesh_shape, tokens, expert_ids, route_weights, gate_weight, up_weight, down_weight):
    shards, groups, line = mesh_shape["dp"], mesh_shape["expert"], mesh_shape["blk"]
    local_count, _, hidden_count = gate_weight.shape
    group = lax.axis_index("expert").astype(jnp.int32).reshape(1)
    line_at = lax.axis_index("blk")
    odd = lax.axis_index("dp") % 2
    place = jnp.where(odd == 1, line - 1 - line_at, line_at).astype(jnp.int32).reshape(1)
    ids, choice_weights = expert_ids.T, route_weights.T
    swap = [(0, 1), (1, 0)]

    def hop(value, source, target):
        pairs = []
        for shard in range(shards):
            ends = (line - 1 - source, line - 1 - target) if shard % 2 else (source, target)
            pairs.append((shard * line + ends[0], shard * line + ends[1]))
        return lax.ppermute(value, ("dp", "blk"), pairs)

    rows = pick(group, ids, tokens, local_count)
    if shards == 2:
        rows = [rows, lax.ppermute(rows, "dp", swap)]
    else:
        rows = [lax.all_gather(rows, "dp", axis=1, tiled=True)]
    row_counts = [part.shape[1] for part in rows]

    widths = chunk_widths(hidden_count)
    starts = [sum(widths[:c]) for c in range(len(widths))]
    full, short, values, got, totals, after = {}, {}, {}, {}, [], []
    for name, c in ORDER:
        if c >= len(widths):
            continue
        kind = CHUNKS[c][1]
        owner, summed_by = OWNER[kind]
        chunks, way = GROUPS.get(c, ((), ""))
        chunks = [q for q in chunks if q < len(widths)]
        if name == "g":
            full[c], short[c] = gate_up(
                place, rows, (gate_weight, up_weight), starts[c], widths[c], after
            )
            after = [full[c]]
        elif name == "h":
            arrived = [[got[m, q] for m in summed_by] for q in chunks]
            values[c] = hidden_values(place, owner, [full[q] for q in chunks], arrived, after)
            after = [values[c]]
        elif name == "d":
            totals = down(
                place,
                [values[c] if m is None else got[m, c] for m in HELD[kind]],
                down_weight,
                [starts[q] for q in chunks],
                [widths[q] for q in chunks],
                totals,
                row_counts,
                after,
            )
            after = [totals[0]]
        else:
            route = SUMS[kind] if name[0] == "m" else BACK[kind, way]
            source, target, needed = route[name]
            if name == "m0":
                sent = short[c]
            elif name == "mb":
                sent = round_to_send(place, source, full[c], after)
                after = [sent]
            elif name[0] == "m":
                sent = add_to_send(place, source, full[c], got[needed, c], after)
                after = [sent]
            elif needed is None:
                sent = values[c]
            else:
                sent = got[needed, c] = pass_on(got[needed, c], after)
                after = [sent]
            got[name, c] = hop(sent, source, target)

    if shards == 2:
        sums = [totals[0], lax.ppermute(totals[1], "dp", swap)]
    else:
        sums = [lax.psum_scatter(totals[0], "dp", scatter_dimension=1, tiled=True)]
    own, *sent = combine(group, ids, choice_weights, sums, groups)
    for step in range(groups - 1, 0, -1):
        exchange = [(i, i ^ step) for i in range(groups)]
        own = own + lax.ppermute(sent[step - 1], "expert", exchange).astype(F32)
    block = own.astype(BF16)
    pieces = [block]
    for step in range(1, groups):
        pieces.append(lax.ppermute(block, "expert", [(i, i ^ step) for i in range(groups)]))
    return place_blocks(group, pieces)


def solution(mesh):
    placed = (
        P("dp", "blk"),
        P("dp", None),
        P("dp", None),
        P("expert", "blk", "dp"),
        P("expert", "blk", "dp"),
        P("expert", "dp", "blk"),
    )
    return jax.shard_map(
        functools.partial(local, dict(mesh.shape)),
        mesh=mesh,
        in_specs=placed,
        out_specs=P("dp", "blk"),
        check_vma=False,
    )
```
